32 devices in a mesh: tm: 2 (over x), ha: 4 (over z), wa: 4 (over y, core).
Axes of the slice: x: 2, y: 2, z: 4, core: 2. Of those that a mesh axis runs over, the one named last changes fastest.
Arguments:
- frames: bfloat16 [2, 128, 256, 128], P('tm', 'ha', 'wa'), may hold values from -24 to 24
- conv_first: bfloat16 [3, 3, 128, 128], replicated, may hold values from -0.1875 to 0.1875
- conv_second: bfloat16 [3, 3, 128, 128], replicated, may hold values from -0.1875 to 0.1875
- norm_attn: float32 [128], replicated, may hold values from 0.25 to 1.75
- qkv_weight: bfloat16 [128, 384], replicated, may hold values from -0.81 to 0.81
- out_weight: bfloat16 [128, 128], replicated, may hold values from -0.5 to 0.5
- norm_mlp: float32 [128], replicated, may hold values from 0.25 to 1.75
- mlp_in: bfloat16 [128, 512], replicated, may hold values from -0.5 to 0.5
- mlp_out: bfloat16 [512, 128], replicated, may hold values from -0.25 to 0.25
- target: bfloat16 [128, 256, 2, 128], P(('ha', 'tm'), 'wa'), may hold values from -18 to 18
Outputs:
- predicted: bfloat16 [128, 256, 2, 128], P(('ha', 'tm'), 'wa')
- loss: float32 [], replicated
The draws below stay inside these ranges and needn't reach their ends.
All inputs are finite; a program needn't handle non-finite values.
Results may differ from the reference program's by a relative error of at most 0.014.
Values may be sent and summed in bfloat16 or wider, within the bound.
A program may use at most 128 MiB of HBM per device.

```python
import jax
import jax.numpy as jnp
from jax import lax

C = 128
HID = 512
HEADS = 4
RADIUS = 4
TH = 32
FRAMES = 2
H = 128
W = 256


def draw_frames(key, part):
    base_key = jax.random.fold_in(jax.random.fold_in(key, 17), 0)
    values = jax.random.normal(base_key, (FRAMES, H, W, C), jnp.float32)
    values = jnp.clip(values, -6.0, 6.0)
    return values.astype(jnp.bfloat16)


def draw_norm_attn(key, part):
    gain_key = jax.random.fold_in(jax.random.fold_in(key, 31), 0)
    values = 1.0 + 0.15 * jnp.clip(jax.random.normal(gain_key, (C,), jnp.float32), -5.0, 5.0)
    return values.astype(jnp.float32)


def draw_qkv_weight(key, part):
    weight_key = jax.random.fold_in(jax.random.fold_in(key, 29), 0)
    values = jnp.clip(jax.random.normal(weight_key, (C, 3 * C), jnp.float32), -4.0, 4.0) * C ** (-0.5)
    return values.astype(jnp.bfloat16)


def draw_target(key, part):
    noise_key = jax.random.fold_in(key, 53)
    values = jnp.clip(jax.random.normal(noise_key, (H, W, FRAMES, C), jnp.float32), -6.0, 6.0)
    inner = (jnp.arange(H) % TH).astype(jnp.float32) / TH
    across = jnp.arange(W).astype(jnp.float32) / W
    row_scale = 0.5 + inner
    col_scale = 0.6 + 0.8 * across
    scale = row_scale[:, None, None, None] * col_scale[None, :, None, None]
    return (values * scale).astype(jnp.bfloat16)


def normal_values(rng, extent, spread, most, held_as=jnp.bfloat16):
    return jnp.clip(spread * jax.random.normal(rng, extent, jnp.float32), -most, most).astype(held_as)


def setup_inputs(seed: int = 0) -> dict:
    key_of = jax.random.split(jax.random.key(seed), 11)
    return {
        "frames": draw_frames(jax.random.fold_in(key_of[10], 71), 0),
        "conv_first": normal_values(key_of[1], (3, 3, C, C), (9 * C) ** -0.5, 0.1875),
        "conv_second": normal_values(key_of[2], (3, 3, C, C), (9 * C) ** -0.5, 0.1875),
        "norm_attn": draw_norm_attn(jax.random.fold_in(key_of[10], 71), 0),
        "qkv_weight": draw_qkv_weight(jax.random.fold_in(key_of[10], 71), 0),
        "out_weight": normal_values(key_of[5], (C, C), C ** -0.5, 0.5),
        "norm_mlp": jnp.clip(1.0 + 0.15 * jax.random.normal(key_of[6], (C,), jnp.float32), 0.25, 1.75),
        "mlp_in": normal_values(key_of[7], (C, HID), C ** -0.5, 0.5),
        "mlp_out": normal_values(key_of[8], (HID, C), HID ** -0.5, 0.25),
        "target": draw_target(jax.random.fold_in(key_of[10], 71), 0),
    }


EPSILON = 1e-06

def convolve(padded, kernel, row_count, col_count):
    summed = jnp.zeros((row_count * col_count, kernel.shape[3]), jnp.float32)
    for tap_row in range(3):
        for tap_col in range(3):
            patch = padded[tap_row:tap_row + row_count, tap_col:tap_col + col_count]
            summed = summed + jnp.dot(patch.reshape(-1, patch.shape[2]), kernel[tap_row, tap_col], preferred_element_type=jnp.float32)
    return summed.reshape(row_count, col_count, -1)

def encode_frame(current, following, conv_first, conv_second):
    span = 2 * RADIUS + 1
    windowed = jnp.pad(following, ((RADIUS, RADIUS), (RADIUS, RADIUS), (0, 0))).astype(jnp.float32)
    current_f = current.astype(jnp.float32)
    scores = []
    for shift_row in range(span):
        for shift_col in range(span):
            scores.append(lax.optimization_barrier(jnp.sum(current_f * windowed[shift_row:shift_row + H, shift_col:shift_col + W], axis=-1)))
    scores = jnp.stack(scores, axis=-1) * C ** (-0.5)
    top = lax.optimization_barrier(jnp.max(scores, axis=-1, keepdims=True))
    expo = jnp.exp(scores - top)
    probs = (expo / lax.optimization_barrier(jnp.sum(expo, axis=-1, keepdims=True))).astype(jnp.bfloat16).astype(jnp.float32)
    gathered = jnp.zeros((H, W, C), jnp.float32)
    for shift_row in range(span):
        for shift_col in range(span):
            slot = shift_row * span + shift_col
            gathered = gathered + probs[:, :, slot:slot + 1] * windowed[shift_row:shift_row + H, shift_col:shift_col + W]
    blended = (current_f + gathered).astype(jnp.bfloat16)
    hidden_map = jax.nn.gelu(convolve(jnp.pad(blended, ((1, 1), (1, 1), (0, 0))), conv_first, H, W)).astype(jnp.bfloat16)
    encoded = blended.astype(jnp.float32) + convolve(jnp.pad(hidden_map, ((1, 1), (1, 1), (0, 0))), conv_second, H, W)
    return encoded.astype(jnp.bfloat16)

def predict_row(series, norm_attn, qkv_weight, out_weight, norm_mlp, mlp_in, mlp_out):
    npos, nframes, chans = series.shape
    depth = chans // HEADS
    base = series.astype(jnp.float32)
    normed = (base * lax.rsqrt(lax.optimization_barrier(jnp.mean(base * base, axis=-1, keepdims=True)) + EPSILON) * norm_attn).astype(jnp.bfloat16)
    projected = jnp.dot(normed.reshape(-1, chans), qkv_weight, preferred_element_type=jnp.float32).astype(jnp.bfloat16)
    projected = projected.reshape(npos, nframes, 3, HEADS, depth).astype(jnp.float32)
    queries, key_rows, value_rows = (projected[:, :, 0], projected[:, :, 1], projected[:, :, 2])
    scores = jnp.einsum('nqhd,nkhd->nhqk', queries, key_rows) * depth ** (-0.5)
    frame_ids = jnp.arange(nframes)
    allowed = frame_ids[None, :] <= frame_ids[:, None]
    scores = jnp.where(allowed, scores, -1e+30)
    top = lax.optimization_barrier(jnp.max(scores, axis=-1, keepdims=True))
    expo = jnp.exp(scores - top)
    weights = (expo / lax.optimization_barrier(jnp.sum(expo, axis=-1, keepdims=True))).astype(jnp.bfloat16).astype(jnp.float32)
    attended = jnp.einsum('nhqk,nkhd->nqhd', weights, value_rows).reshape(npos, nframes, chans).astype(jnp.bfloat16)
    resid = base + jnp.dot(attended.reshape(-1, chans), out_weight, preferred_element_type=jnp.float32).reshape(npos, nframes, chans)
    mlp_input = (resid * lax.rsqrt(lax.optimization_barrier(jnp.mean(resid * resid, axis=-1, keepdims=True)) + EPSILON) * norm_mlp).astype(jnp.bfloat16)
    mlp_hidden = jax.nn.gelu(jnp.dot(mlp_input.reshape(-1, chans), mlp_in, preferred_element_type=jnp.float32)).astype(jnp.bfloat16)
    output = resid + jnp.dot(mlp_hidden, mlp_out, preferred_element_type=jnp.float32).reshape(npos, nframes, chans)
    return output.astype(jnp.bfloat16)

def reference(frames, conv_first, conv_second, norm_attn, qkv_weight, out_weight, norm_mlp, mlp_in, mlp_out, target):
    following = jnp.concatenate([frames[1:], jnp.zeros((1, H, W, C), jnp.bfloat16)], axis=0)
    encoded = lax.map(lambda pair: encode_frame(pair[0], pair[1], conv_first, conv_second), (frames, following))
    series = jnp.transpose(encoded, (1, 2, 0, 3))
    predicted = lax.map(lambda row: predict_row(row, norm_attn, qkv_weight, out_weight, norm_mlp, mlp_in, mlp_out), series)
    errors = predicted.astype(jnp.float32) - target.astype(jnp.float32)
    loss = jnp.sum(errors * errors) / (H * W * FRAMES * C)
    return (predicted, loss)
```

```python
import jax
import jax.numpy as jnp
from jax import lax
from jax.experimental import pallas as pl
from jax.experimental.pallas import tpu as pltpu
from jax.sharding import PartitionSpec as P

HEADS = 4
RADIUS = 4


EPSILON = 1e-06


def shifted(value, axis, steps):
    count = lax.axis_size(axis)
    initial, last = (max(0, -steps), min(count, count - steps))
    return lax.ppermute(value, axis, [(source, source + steps) for source in range(initial, last)])


def with_halo(block, sides, width):
    for axis, dim in sides:
        count = lax.axis_size(axis)
        forward = [(i, i + 1) for i in range(count - 1)]
        backward = [(target, source) for source, target in forward]
        low = lax.ppermute(
            lax.slice_in_dim(block, block.shape[dim] - width, None, axis=dim), axis, forward
        )
        high = lax.ppermute(lax.slice_in_dim(block, 0, width, axis=dim), axis, backward)
        block = jnp.concatenate([low, block, high], axis=dim)
    return block


def convolve(padded, kernel, row_count, col_count):
    nframes = padded.shape[0]
    summed = jnp.zeros((nframes * row_count * col_count, kernel.shape[3]), jnp.float32)
    for tap_row in range(3):
        for tap_col in range(3):
            patch = padded[:, tap_row : tap_row + row_count, tap_col : tap_col + col_count]
            summed = summed + jnp.dot(
                patch.reshape(-1, patch.shape[3]),
                kernel[tap_row, tap_col],
                preferred_element_type=jnp.float32,
            )
    return summed.reshape(nframes, row_count, col_count, -1)


def correlate(current, windowed):
    nframes, tile_rows, tile_cols, channels = current.shape
    span = 2 * RADIUS + 1
    reach = tile_cols + 2 * RADIUS
    col_here = jnp.arange(tile_cols)[:, None, None]
    col_there = jnp.arange(reach)[None, :, None]
    offsets = jnp.arange(span)[None, None, :]
    band = col_there == col_here + offsets
    band_f32 = band.astype(jnp.float32)
    band_bf16 = band.astype(jnp.bfloat16)
    pieces = []
    for shift_row in range(span):
        rows_window = windowed[:, shift_row : shift_row + tile_rows]
        banded = jnp.einsum(
            "fhic,fhjc->fhij", current, rows_window, preferred_element_type=jnp.float32
        )
        pieces.append(
            jnp.einsum("fhij,ijb->fhib", banded, band_f32, precision=lax.Precision.HIGHEST)
        )
    scores = jnp.concatenate(pieces, axis=-1) * channels ** (-0.5)
    top = jnp.max(scores, axis=-1, keepdims=True)
    expo = jnp.exp(scores - top)
    probs = (expo / jnp.sum(expo, axis=-1, keepdims=True)).astype(jnp.bfloat16)
    gathered = jnp.zeros(current.shape, jnp.float32)
    for shift_row in range(span):
        rows_window = windowed[:, shift_row : shift_row + tile_rows]
        chosen = probs[..., shift_row * span : (shift_row + 1) * span]
        spread = jnp.einsum(
            "fhib,ijb->fhij", chosen, band_bf16, preferred_element_type=jnp.float32
        ).astype(jnp.bfloat16)
        gathered = gathered + jnp.einsum(
            "fhij,fhjc->fhic", spread, rows_window, preferred_element_type=jnp.float32
        )
    return (current.astype(jnp.float32) + gathered).astype(jnp.bfloat16)


def project(series, norm_attn, qkv_weight):
    npos, nframes, channels = series.shape
    base = series.astype(jnp.float32)
    normed = (
        base * lax.rsqrt(jnp.mean(base * base, axis=-1, keepdims=True) + EPSILON) * norm_attn
    ).astype(jnp.bfloat16)
    projected = jnp.dot(
        normed.reshape(-1, channels), qkv_weight, preferred_element_type=jnp.float32
    ).astype(jnp.bfloat16)
    projected = projected.reshape(npos, nframes, 3 * channels)
    return (
        projected[..., :channels],
        projected[..., channels : 2 * channels],
        projected[..., 2 * channels :],
    )


def attend(queries, key_rows, value_rows, query_ids, key_ids):
    npos, query_count, channels = queries.shape
    key_count = key_rows.shape[1]
    depth = channels // HEADS
    query_heads = queries.reshape(npos, query_count, HEADS, depth)
    key_heads = key_rows.reshape(npos, key_count, HEADS, depth)
    value_heads = value_rows.reshape(npos, key_count, HEADS, depth)
    scores = jnp.einsum(
        "pqhd,pkhd->phqk", query_heads, key_heads, preferred_element_type=jnp.float32
    ) * depth ** (-0.5)
    allowed = key_ids[None, :] <= query_ids[:, None]
    scores = jnp.where(allowed, scores, -1e30)
    top = jnp.max(scores, axis=-1, keepdims=True)
    expo = jnp.exp(scores - top)
    weights = (expo / jnp.sum(expo, axis=-1, keepdims=True)).astype(jnp.bfloat16)
    attended = jnp.einsum(
        "phqk,pkhd->pqhd", weights, value_heads, preferred_element_type=jnp.float32
    )
    return attended.reshape(npos, query_count, channels).astype(jnp.bfloat16)


def finish(series, attended, out_weight, norm_mlp, mlp_in, mlp_out):
    npos, nframes, channels = series.shape
    resid = series.astype(jnp.float32) + jnp.dot(
        attended.reshape(-1, channels), out_weight, preferred_element_type=jnp.float32
    ).reshape(npos, nframes, channels)
    mlp_input = (
        resid * lax.rsqrt(jnp.mean(resid * resid, axis=-1, keepdims=True) + EPSILON) * norm_mlp
    ).astype(jnp.bfloat16)
    mlp_hidden = jax.nn.gelu(
        jnp.dot(mlp_input.reshape(-1, channels), mlp_in, preferred_element_type=jnp.float32)
    ).astype(jnp.bfloat16)
    output = resid + jnp.dot(mlp_hidden, mlp_out, preferred_element_type=jnp.float32).reshape(
        npos, nframes, channels
    )
    return output.astype(jnp.bfloat16)


def shards(
    frames,
    conv_first,
    conv_second,
    norm_attn,
    qkv_weight,
    out_weight,
    norm_mlp,
    mlp_in,
    mlp_out,
    target,
):
    frame_count, tile_rows, tile_cols, channels = frames.shape
    arrival = shifted(frames, "tm", -1)
    following = jnp.concatenate([frames[1:], arrival], axis=0)
    windowed = with_halo(following, (("ha", 1), ("wa", 2)), RADIUS)
    blended = correlate(frames, windowed)
    padded_first = with_halo(blended, (("ha", 1), ("wa", 2)), 1)
    hidden_map = jax.nn.gelu(convolve(padded_first, conv_first, tile_rows, tile_cols)).astype(
        jnp.bfloat16
    )
    hidden_map = with_halo(hidden_map, (("ha", 1), ("wa", 2)), 1)
    encoded = (
        blended.astype(jnp.float32) + convolve(hidden_map, conv_second, tile_rows, tile_cols)
    ).astype(jnp.bfloat16)
    series = jnp.transpose(
        lax.all_to_all(encoded, "tm", split_axis=1, concat_axis=0, tiled=True), (1, 2, 0, 3)
    )
    layout = series.shape
    tokens_flat = series.reshape(-1, layout[2], layout[3])
    frame_ids = jnp.arange(layout[2])
    queries, key_rows, value_rows = project(tokens_flat, norm_attn, qkv_weight)
    attended = attend(queries, key_rows, value_rows, frame_ids, frame_ids)
    predicted = finish(tokens_flat, attended, out_weight, norm_mlp, mlp_in, mlp_out).reshape(layout)
    errors = predicted.astype(jnp.float32) - target.astype(jnp.float32)
    summed = lax.psum(jnp.sum(errors * errors), ("tm", "ha", "wa"))
    entries = predicted.size * lax.axis_size("tm") * lax.axis_size("ha") * lax.axis_size("wa")
    return (predicted, summed / entries)


RIMS = (2, RADIUS + 2)
SIDE = 16
QROWS = 10
QCOLS = 16


def window_parts(frame, place, tile_rows, tile_cols):
    rim = RIMS[frame]
    main = tile_rows // 2 + rim
    if place == 0:
        rows = [(0, main, rim, 0), (tile_rows - rim, rim, 0, -1)]
    else:
        rows = [(tile_rows - main, main, 0, 0), (0, rim, main, 1)]
    cols = [
        (0, tile_cols, SIDE, 0),
        (tile_cols - SIDE, SIDE, 0, -1),
        (0, SIDE, SIDE + tile_cols, 1),
    ]
    return [(row, col) for row in rows for col in cols]


def gather_kernel(
    ha_count, wa_count, frames_ref, win0, win1, send_sem, recv_sem
):
    wins = (win0, win1)
    _, tile_rows, tile_cols, _ = frames_ref.shape
    here_t, here_a, here_w = (lax.axis_index(n) for n in ("tm", "ha", "wa"))
    barrier = pltpu.get_barrier_semaphore()

    def inside(a, w):
        return (a >= 0) & (a < ha_count) & (w >= 0) & (w < wa_count)

    def device(t, a, w):
        wrapped = (lax.rem(a + ha_count, ha_count), lax.rem(w + wa_count, wa_count))
        return (jnp.int32(t), *wrapped)

    def branch(mine):
        other = 1 - mine
        expected = jnp.int32(0)
        for frame in range(2):
            for row, col in window_parts(frame, mine, tile_rows, tile_cols):
                a, w = here_a + row[3], here_w + col[3]
                if frame == mine and row[3] == 0 and col[3] == 0:
                    continue

                @pl.when(inside(a, w))
                def _():
                    pl.semaphore_signal(
                        barrier,
                        inc=1,
                        device_id=device(frame, a, w),
                        device_id_type=pl.DeviceIdType.MESH,
                    )

        sends = []
        for place in range(2):
            for slot, (row, col) in enumerate(
                window_parts(mine, place, tile_rows, tile_cols)
            ):
                a, w = here_a - row[3], here_w - col[3]
                local = place == mine and row[3] == 0 and col[3] == 0
                source = frames_ref.at[0, pl.ds(row[0], row[1]), pl.ds(col[0], col[1])]
                target = wins[mine].at[pl.ds(row[2], row[1]), pl.ds(col[2], col[1])]
                if local:
                    own = pltpu.make_async_copy(source, target, recv_sem.at[mine * 6 + slot])
                    continue
                expected = expected + inside(a, w).astype(jnp.int32)
                sends.append(
                    (
                        inside(a, w),
                        pltpu.make_async_remote_copy(
                            src_ref=source,
                            dst_ref=target,
                            send_sem=send_sem.at[place * 6 + slot],
                            recv_sem=recv_sem.at[mine * 6 + slot],
                            device_id=device(place, a, w),
                            device_id_type=pl.DeviceIdType.MESH,
                        ),
                    )
                )
        own.start()
        arrivals = []
        for frame in range(2):
            for slot, (row, col) in enumerate(
                window_parts(frame, mine, tile_rows, tile_cols)
            ):
                a, w = here_a + row[3], here_w + col[3]
                if frame == mine and row[3] == 0 and col[3] == 0:
                    continue
                target = wins[frame].at[pl.ds(row[2], row[1]), pl.ds(col[2], col[1])]

                def clear(target=target):
                    target[...] = jnp.zeros(target.shape, target.dtype)

                arrival = pltpu.make_async_remote_copy(
                    src_ref=target,
                    dst_ref=target,
                    send_sem=send_sem.at[frame * 6 + slot],
                    recv_sem=recv_sem.at[frame * 6 + slot],
                    device_id=device(other, here_a, here_w),
                    device_id_type=pl.DeviceIdType.MESH,
                )
                arrivals.append((inside(a, w), arrival))
                pl.when(jnp.logical_not(inside(a, w)))(clear)
        pl.semaphore_wait(barrier, expected)
        for exists, copy in sends:
            pl.when(exists)(copy.start)
        own.wait()
        for exists, arrival in arrivals:
            pl.when(exists)(arrival.wait_recv)
        for exists, copy in sends:
            pl.when(exists)(copy.wait_send)

    pl.when(here_t == 0)(lambda: branch(0))
    pl.when(here_t == 1)(lambda: branch(1))


def gather_windows(frames):
    _, tile_rows, tile_cols, channels = frames.shape
    shapes = [
        jax.ShapeDtypeStruct(
            (tile_rows // 2 + 2 * rim, tile_cols + 2 * SIDE, channels), frames.dtype
        )
        for rim in RIMS
    ]
    ha_count, wa_count = lax.axis_size("ha"), lax.axis_size("wa")

    def kernel(*refs):
        gather_kernel(ha_count, wa_count, *refs)

    return pl.pallas_call(
        kernel,
        out_shape=shapes,
        in_specs=[pl.BlockSpec(memory_space=pl.ANY)],
        out_specs=[pl.BlockSpec(memory_space=pltpu.VMEM)] * 2,
        scratch_shapes=[
            pltpu.SemaphoreType.DMA((12,)),
            pltpu.SemaphoreType.DMA((12,)),
        ],
        compiler_params=pltpu.CompilerParams(collective_id=0, has_side_effects=True),
    )(frames)


def rounded(value):
    return value.astype(jnp.bfloat16)


def predict_kernel(
    ha_count,
    wa_count,
    win0,
    win1,
    conv_first,
    conv_second,
    norm_attn,
    qkv_weight,
    out_weight,
    norm_mlp,
    mlp_in,
    mlp_out,
    target,
    predicted,
    loss,
    bias,
    blended,
    patches,
    hidden,
    patches_hidden,
    encoded,
    paired,
):
    row_count = win0.shape[0] - 2 * RIMS[0]
    width = win0.shape[1]
    col_count = width - 2 * SIDE
    channels = win0.shape[2]
    here_t, here_a, here_w = (lax.axis_index(n) for n in ("tm", "ha", "wa"))
    first_row = (here_a * 2 + here_t) * row_count
    first_col = here_w * col_count
    image_rows = ha_count * 2 * row_count
    image_cols = wa_count * col_count

    def in_image(shape, row_start, col_start):
        row = lax.broadcasted_iota(jnp.int32, shape, 0) + row_start
        col = lax.broadcasted_iota(jnp.int32, shape, 1) + col_start
        return (row >= 0) & (row < image_rows) & (col >= 0) & (col < image_cols)

    krows, kcols = QROWS + 2 * RADIUS, QCOLS + 16
    queries_n, keys_n = QROWS * QCOLS, krows * kcols
    q_at = lax.broadcasted_iota(jnp.int32, (queries_n, keys_n), 0)
    k_at = lax.broadcasted_iota(jnp.int32, (queries_n, keys_n), 1)
    d_row = k_at // kcols - q_at // QCOLS
    d_col = k_at % kcols - q_at % QCOLS - (8 - RADIUS)
    near = (d_row >= 0) & (d_row <= 2 * RADIUS) & (d_col >= 0) & (d_col <= 2 * RADIUS)
    bias[...] = jnp.where(near, 0.0, -1e30)
    scale = channels ** (-0.5) * 1.4426950408889634

    @pl.loop(0, win0.shape[0] // QROWS)
    def _(step):
        top_row = step * QROWS
        for start in range(8, width - 8, QCOLS):
            query = win0[pl.ds(top_row, QROWS), start : start + QCOLS].reshape(
                queries_n, channels
            )
            keys = win1[pl.ds(top_row, krows), start - 8 : start + QCOLS + 8].reshape(
                keys_n, channels
            )
            scores = lax.dot_general(
                query, keys, (((1,), (1,)), ((), ())), preferred_element_type=jnp.float32
            )
            scores = scores * scale + bias[...]
            expo = jnp.exp2(scores - jnp.max(scores, axis=-1, keepdims=True))
            total = jnp.sum(expo, axis=-1, keepdims=True)
            found = jnp.dot(rounded(expo), keys, preferred_element_type=jnp.float32) / total
            mixed = rounded(query.astype(jnp.float32) + found).astype(jnp.float32)
            mixed = mixed.reshape(QROWS, QCOLS, channels)
            keep = in_image(
                mixed.shape, first_row - RIMS[0] + top_row, first_col - SIDE + start
            )
            blended[pl.ds(top_row, QROWS), start : start + QCOLS] = jnp.where(keep, mixed, 0.0)

    for frame in range(2):
        if frame == 1:
            gap = RIMS[1] - RIMS[0]
            blended[...] = win1[gap : gap + win0.shape[0]].astype(jnp.float32)
        for tap in range(3):
            patches[:, :, tap * channels : (tap + 1) * channels] = rounded(
                blended[:, 7 + tap : width - 9 + tap]
            )

        @pl.loop(0, (row_count + 2) // 6)
        def _(step):
            at = step * 6
            lhs = jnp.concatenate([patches[pl.ds(at + i, 6)] for i in range(3)], axis=-1)
            shape = (6, width - 16, channels)
            out = jnp.dot(
                lhs.reshape(-1, 9 * channels), conv_first[...], preferred_element_type=jnp.float32
            )
            out = rounded(jax.nn.gelu(out)).astype(jnp.float32).reshape(shape)
            keep = in_image(shape, first_row - 1 + at, first_col - 8)
            hidden[pl.ds(at, 6)] = jnp.where(keep, out, 0.0)

        for tap in range(3):
            patches_hidden[:, :, tap * channels : (tap + 1) * channels] = rounded(
                hidden[:, 7 + tap : 7 + tap + col_count]
            )

        @pl.loop(0, row_count // 8)
        def _(step):
            at = step * 8
            lhs = jnp.concatenate([patches_hidden[pl.ds(at + i, 8)] for i in range(3)], axis=-1)
            out = jnp.dot(
                lhs.reshape(-1, 9 * channels), conv_second[...], preferred_element_type=jnp.float32
            )
            base = blended[pl.ds(at + 2, 8), SIDE : SIDE + col_count].reshape(out.shape)
            encoded[frame, pl.ds(at * col_count, 8 * col_count)] = rounded(base + out).astype(
                jnp.float32
            )

    depth = channels // HEADS
    lane_in = lax.broadcasted_iota(jnp.int32, (2 * channels, channels), 0) % channels
    lane_out = lax.broadcasted_iota(jnp.int32, (2 * channels, channels), 1)
    head_sum = rounded(jnp.where(lane_in // depth == lane_out // depth, 1.0, 0.0))
    chunk = 256

    def unit(value, gain):
        mean = jnp.mean(value * value, axis=-1, keepdims=True)
        return rounded(value * lax.rsqrt(mean + EPSILON) * gain[...])

    def dot(left, right):
        return jnp.dot(left, right, preferred_element_type=jnp.float32)

    @pl.loop(0, row_count * col_count // chunk, init_carry=jnp.zeros((8, channels), jnp.float32))
    def errors(step, carry):
        at = pl.multiple_of(step * chunk, chunk)
        series = jnp.concatenate([encoded[0, pl.ds(at, chunk)], encoded[1, pl.ds(at, chunk)]])
        projected = rounded(dot(unit(series, norm_attn), qkv_weight[...])).astype(jnp.float32)
        query = projected[chunk:, :channels]
        keys = projected[:, channels : 2 * channels]
        values = projected[:, 2 * channels :]
        product = query * (keys[chunk:] - keys[:chunk])
        high = rounded(product)
        low = rounded(product - high.astype(jnp.float32))
        gap = dot(jnp.concatenate([high, low], axis=-1), head_sum) * depth ** (-0.5)
        half = 0.5 * jnp.tanh(0.5 * gap)
        weight_now = rounded(0.5 + half).astype(jnp.float32)
        weight_past = rounded(0.5 - half).astype(jnp.float32)
        attended = weight_past * values[:chunk] + weight_now * values[chunk:]
        attended = rounded(jnp.concatenate([values[:chunk], attended]))
        resid = series + dot(attended, out_weight[...])
        inner = rounded(jax.nn.gelu(dot(unit(resid, norm_mlp), mlp_in[...])))
        output = resid + dot(inner, mlp_out[...])
        paired[pl.ds(0, chunk, stride=2)] = output[:chunk]
        paired[pl.ds(1, chunk, stride=2)] = output[chunk:]
        final = rounded(paired[...])
        both = pl.ds(pl.multiple_of(2 * at, 2 * chunk), 2 * chunk)
        predicted[both] = final
        error = final.astype(jnp.float32) - target[both].astype(jnp.float32)
        return carry + jnp.sum((error * error).reshape(-1, 8, channels), axis=0)

    loss[...] = errors


def predict(win0, win1, weights, target):
    row_count = win0.shape[0] - 2 * RIMS[0]
    width, channels = win0.shape[1:]
    col_count = width - 2 * SIDE
    ha_count, wa_count = lax.axis_size("ha"), lax.axis_size("wa")

    def kernel(*refs):
        predict_kernel(ha_count, wa_count, *refs)

    tokens = 2 * row_count * col_count
    operands = (win0, win1, *weights, target)
    return pl.pallas_call(
        kernel,
        out_shape=[
            jax.ShapeDtypeStruct((tokens, channels), jnp.bfloat16),
            jax.ShapeDtypeStruct((8, channels), jnp.float32),
        ],
        in_specs=[pl.BlockSpec(memory_space=pltpu.VMEM)] * len(operands),
        out_specs=[pl.BlockSpec(memory_space=pltpu.VMEM)] * 2,
        scratch_shapes=[
            pltpu.VMEM((QROWS * QCOLS, (QROWS + 2 * RADIUS) * (QCOLS + 16)), jnp.float32),
            pltpu.VMEM((row_count + 4, width, channels), jnp.float32),
            pltpu.VMEM((row_count + 4, width - 16, 3 * channels), jnp.bfloat16),
            pltpu.VMEM((row_count + 2, width - 16, channels), jnp.float32),
            pltpu.VMEM((row_count + 2, col_count, 3 * channels), jnp.bfloat16),
            pltpu.VMEM((2, row_count * col_count, channels), jnp.float32),
            pltpu.VMEM((512, channels), jnp.float32),
        ],
        compiler_params=pltpu.CompilerParams(vmem_limit_bytes=48 * 1024 * 1024),
    )(*operands)


def pair_shards(
    frames,
    conv_first,
    conv_second,
    norm_attn,
    qkv_weight,
    out_weight,
    norm_mlp,
    mlp_in,
    mlp_out,
    target,
):
    channels = frames.shape[3]
    win0, win1 = gather_windows(frames)
    weights = (
        conv_first.reshape(-1, channels),
        conv_second.reshape(-1, channels),
        norm_attn.reshape(1, channels),
        qkv_weight,
        out_weight,
        norm_mlp.reshape(1, channels),
        mlp_in,
        mlp_out,
    )
    predicted, errors = predict(win0, win1, weights, target.reshape(-1, channels))
    summed = lax.psum(jnp.sum(errors), ("tm", "ha", "wa"))
    entries = target.size * lax.axis_size("tm") * lax.axis_size("ha") * lax.axis_size("wa")
    return (predicted.reshape(target.shape), summed / entries)


def solution(mesh):
    in_specs = (
        P("tm", "ha", "wa", None),
        P(),
        P(),
        P(),
        P(),
        P(),
        P(),
        P(),
        P(),
        P(("ha", "tm"), "wa", None, None),
    )
    out_specs = (P(("ha", "tm"), "wa", None, None), P())
    body = pair_shards if mesh.shape["tm"] == 2 else shards
    return jax.shard_map(body, mesh=mesh, in_specs=in_specs, out_specs=out_specs, check_vma=False)
```

```python
import jax
import jax.numpy as jnp
from jax import lax
from jax.experimental import pallas as pl
from jax.experimental.pallas import tpu as pltpu
from jax.sharding import PartitionSpec as P

HEADS = 4
RADIUS = 4


EPSILON = 1e-06


def shifted(value, axis, steps):
    count = lax.axis_size(axis)
    initial, last = (max(0, -steps), min(count, count - steps))
    return lax.ppermute(value, axis, [(source, source + steps) for source in range(initial, last)])


def with_halo(block, sides, width):
    for axis, dim in sides:
        count = lax.axis_size(axis)
        forward = [(i, i + 1) for i in range(count - 1)]
        backward = [(target, source) for source, target in forward]
        low = lax.ppermute(
            lax.slice_in_dim(block, block.shape[dim] - width, None, axis=dim), axis, forward
        )
        high = lax.ppermute(lax.slice_in_dim(block, 0, width, axis=dim), axis, backward)
        block = jnp.concatenate([low, block, high], axis=dim)
    return block


def convolve(padded, kernel, row_count, col_count):
    nframes = padded.shape[0]
    summed = jnp.zeros((nframes * row_count * col_count, kernel.shape[3]), jnp.float32)
    for tap_row in range(3):
        for tap_col in range(3):
            patch = padded[:, tap_row : tap_row + row_count, tap_col : tap_col + col_count]
            summed = summed + jnp.dot(
                patch.reshape(-1, patch.shape[3]),
                kernel[tap_row, tap_col],
                preferred_element_type=jnp.float32,
            )
    return summed.reshape(nframes, row_count, col_count, -1)


def correlate(current, windowed):
    nframes, tile_rows, tile_cols, channels = current.shape
    span = 2 * RADIUS + 1
    reach = tile_cols + 2 * RADIUS
    col_here = jnp.arange(tile_cols)[:, None, None]
    col_there = jnp.arange(reach)[None, :, None]
    offsets = jnp.arange(span)[None, None, :]
    band = col_there == col_here + offsets
    band_f32 = band.astype(jnp.float32)
    band_bf16 = band.astype(jnp.bfloat16)
    pieces = []
    for shift_row in range(span):
        rows_window = windowed[:, shift_row : shift_row + tile_rows]
        banded = jnp.einsum(
            "fhic,fhjc->fhij", current, rows_window, preferred_element_type=jnp.float32
        )
        pieces.append(
            jnp.einsum("fhij,ijb->fhib", banded, band_f32, precision=lax.Precision.HIGHEST)
        )
    scores = jnp.concatenate(pieces, axis=-1) * channels ** (-0.5)
    top = jnp.max(scores, axis=-1, keepdims=True)
    expo = jnp.exp(scores - top)
    probs = (expo / jnp.sum(expo, axis=-1, keepdims=True)).astype(jnp.bfloat16)
    gathered = jnp.zeros(current.shape, jnp.float32)
    for shift_row in range(span):
        rows_window = windowed[:, shift_row : shift_row + tile_rows]
        chosen = probs[..., shift_row * span : (shift_row + 1) * span]
        spread = jnp.einsum(
            "fhib,ijb->fhij", chosen, band_bf16, preferred_element_type=jnp.float32
        ).astype(jnp.bfloat16)
        gathered = gathered + jnp.einsum(
            "fhij,fhjc->fhic", spread, rows_window, preferred_element_type=jnp.float32
        )
    return (current.astype(jnp.float32) + gathered).astype(jnp.bfloat16)


def project(series, norm_attn, qkv_weight):
    npos, nframes, channels = series.shape
    base = series.astype(jnp.float32)
    normed = (
        base * lax.rsqrt(jnp.mean(base * base, axis=-1, keepdims=True) + EPSILON) * norm_attn
    ).astype(jnp.bfloat16)
    projected = jnp.dot(
        normed.reshape(-1, channels), qkv_weight, preferred_element_type=jnp.float32
    ).astype(jnp.bfloat16)
    projected = projected.reshape(npos, nframes, 3 * channels)
    return (
        projected[..., :channels],
        projected[..., channels : 2 * channels],
        projected[..., 2 * channels :],
    )


def attend(queries, key_rows, value_rows, query_ids, key_ids):
    npos, query_count, channels = queries.shape
    key_count = key_rows.shape[1]
    depth = channels // HEADS
    query_heads = queries.reshape(npos, query_count, HEADS, depth)
    key_heads = key_rows.reshape(npos, key_count, HEADS, depth)
    value_heads = value_rows.reshape(npos, key_count, HEADS, depth)
    scores = jnp.einsum(
        "pqhd,pkhd->phqk", query_heads, key_heads, preferred_element_type=jnp.float32
    ) * depth ** (-0.5)
    allowed = key_ids[None, :] <= query_ids[:, None]
    scores = jnp.where(allowed, scores, -1e30)
    top = jnp.max(scores, axis=-1, keepdims=True)
    expo = jnp.exp(scores - top)
    weights = (expo / jnp.sum(expo, axis=-1, keepdims=True)).astype(jnp.bfloat16)
    attended = jnp.einsum(
        "phqk,pkhd->pqhd", weights, value_heads, preferred_element_type=jnp.float32
    )
    return attended.reshape(npos, query_count, channels).astype(jnp.bfloat16)


def finish(series, attended, out_weight, norm_mlp, mlp_in, mlp_out):
    npos, nframes, channels = series.shape
    resid = series.astype(jnp.float32) + jnp.dot(
        attended.reshape(-1, channels), out_weight, preferred_element_type=jnp.float32
    ).reshape(npos, nframes, channels)
    mlp_input = (
        resid * lax.rsqrt(jnp.mean(resid * resid, axis=-1, keepdims=True) + EPSILON) * norm_mlp
    ).astype(jnp.bfloat16)
    mlp_hidden = jax.nn.gelu(
        jnp.dot(mlp_input.reshape(-1, channels), mlp_in, preferred_element_type=jnp.float32)
    ).astype(jnp.bfloat16)
    output = resid + jnp.dot(mlp_hidden, mlp_out, preferred_element_type=jnp.float32).reshape(
        npos, nframes, channels
    )
    return output.astype(jnp.bfloat16)


def shards(
    frames,
    conv_first,
    conv_second,
    norm_attn,
    qkv_weight,
    out_weight,
    norm_mlp,
    mlp_in,
    mlp_out,
    target,
):
    frame_count, tile_rows, tile_cols, channels = frames.shape
    arrival = shifted(frames, "tm", -1)
    following = jnp.concatenate([frames[1:], arrival], axis=0)
    windowed = with_halo(following, (("ha", 1), ("wa", 2)), RADIUS)
    blended = correlate(frames, windowed)
    padded_first = with_halo(blended, (("ha", 1), ("wa", 2)), 1)
    hidden_map = jax.nn.gelu(convolve(padded_first, conv_first, tile_rows, tile_cols)).astype(
        jnp.bfloat16
    )
    hidden_map = with_halo(hidden_map, (("ha", 1), ("wa", 2)), 1)
    encoded = (
        blended.astype(jnp.float32) + convolve(hidden_map, conv_second, tile_rows, tile_cols)
    ).astype(jnp.bfloat16)
    series = jnp.transpose(
        lax.all_to_all(encoded, "tm", split_axis=1, concat_axis=0, tiled=True), (1, 2, 0, 3)
    )
    layout = series.shape
    tokens_flat = series.reshape(-1, layout[2], layout[3])
    frame_ids = jnp.arange(layout[2])
    queries, key_rows, value_rows = project(tokens_flat, norm_attn, qkv_weight)
    attended = attend(queries, key_rows, value_rows, frame_ids, frame_ids)
    predicted = finish(tokens_flat, attended, out_weight, norm_mlp, mlp_in, mlp_out).reshape(layout)
    errors = predicted.astype(jnp.float32) - target.astype(jnp.float32)
    summed = lax.psum(jnp.sum(errors * errors), ("tm", "ha", "wa"))
    entries = predicted.size * lax.axis_size("tm") * lax.axis_size("ha") * lax.axis_size("wa")
    return (predicted, summed / entries)


RIMS = (2, RADIUS + 2)
SIDE = 16
QROWS = 10
QCOLS = 16


def window_parts(frame, place, tile_rows, tile_cols):
    rim = RIMS[frame]
    main = tile_rows // 2 + rim
    if place == 0:
        rows = [(0, main, rim, 0), (tile_rows - rim, rim, 0, -1)]
    else:
        rows = [(tile_rows - main, main, 0, 0), (0, rim, main, 1)]
    cols = [
        (0, tile_cols, SIDE, 0),
        (tile_cols - SIDE, SIDE, 0, -1),
        (0, SIDE, SIDE + tile_cols, 1),
    ]
    return [(row, col) for row in rows for col in cols]


def gather_kernel(
    ha_count, wa_count, frames_ref, win0, win1, send_sem, recv_sem
):
    wins = (win0, win1)
    _, tile_rows, tile_cols, _ = frames_ref.shape
    here_t, here_a, here_w = (lax.axis_index(n) for n in ("tm", "ha", "wa"))
    barrier = pltpu.get_barrier_semaphore()

    def inside(a, w):
        return (a >= 0) & (a < ha_count) & (w >= 0) & (w < wa_count)

    def device(t, a, w):
        wrapped = (lax.rem(a + ha_count, ha_count), lax.rem(w + wa_count, wa_count))
        return (jnp.int32(t), *wrapped)

    def branch(mine):
        other = 1 - mine
        expected = jnp.int32(0)
        for frame in range(2):
            for row, col in window_parts(frame, mine, tile_rows, tile_cols):
                a, w = here_a + row[3], here_w + col[3]
                if frame == mine and row[3] == 0 and col[3] == 0:
                    continue

                @pl.when(inside(a, w))
                def _():
                    pl.semaphore_signal(
                        barrier,
                        inc=1,
                        device_id=device(frame, a, w),
                        device_id_type=pl.DeviceIdType.MESH,
                    )

        sends = []
        for place in range(2):
            for slot, (row, col) in enumerate(
                window_parts(mine, place, tile_rows, tile_cols)
            ):
                a, w = here_a - row[3], here_w - col[3]
                local = place == mine and row[3] == 0 and col[3] == 0
                source = frames_ref.at[0, pl.ds(row[0], row[1]), pl.ds(col[0], col[1])]
                target = wins[mine].at[pl.ds(row[2], row[1]), pl.ds(col[2], col[1])]
                if local:
                    own = pltpu.make_async_copy(source, target, recv_sem.at[mine * 6 + slot])
                    continue
                expected = expected + inside(a, w).astype(jnp.int32)
                sends.append(
                    (
                        inside(a, w),
                        pltpu.make_async_remote_copy(
                            src_ref=source,
                            dst_ref=target,
                            send_sem=send_sem.at[place * 6 + slot],
                            recv_sem=recv_sem.at[mine * 6 + slot],
                            device_id=device(place, a, w),
                            device_id_type=pl.DeviceIdType.MESH,
                        ),
                    )
                )
        own.start()
        arrivals = []
        for frame in range(2):
            for slot, (row, col) in enumerate(
                window_parts(frame, mine, tile_rows, tile_cols)
            ):
                a, w = here_a + row[3], here_w + col[3]
                if frame == mine and row[3] == 0 and col[3] == 0:
                    continue
                target = wins[frame].at[pl.ds(row[2], row[1]), pl.ds(col[2], col[1])]

                def clear(target=target):
                    target[...] = jnp.zeros(target.shape, target.dtype)

                arrival = pltpu.make_async_remote_copy(
                    src_ref=target,
                    dst_ref=target,
                    send_sem=send_sem.at[frame * 6 + slot],
                    recv_sem=recv_sem.at[frame * 6 + slot],
                    device_id=device(other, here_a, here_w),
                    device_id_type=pl.DeviceIdType.MESH,
                )
                arrivals.append((inside(a, w), arrival))
                pl.when(jnp.logical_not(inside(a, w)))(clear)
        pl.semaphore_wait(barrier, expected)
        for exists, copy in sends:
            pl.when(exists)(copy.start)
        own.wait()
        for exists, arrival in arrivals:
            pl.when(exists)(arrival.wait_recv)
        for exists, copy in sends:
            pl.when(exists)(copy.wait_send)

    pl.when(here_t == 0)(lambda: branch(0))
    pl.when(here_t == 1)(lambda: branch(1))


def gather_windows(frames):
    _, tile_rows, tile_cols, channels = frames.shape
    shapes = [
        jax.ShapeDtypeStruct(
            (tile_rows // 2 + 2 * rim, tile_cols + 2 * SIDE, channels), frames.dtype
        )
        for rim in RIMS
    ]
    ha_count, wa_count = lax.axis_size("ha"), lax.axis_size("wa")

    def kernel(*refs):
        gather_kernel(ha_count, wa_count, *refs)

    return pl.pallas_call(
        kernel,
        out_shape=shapes,
        in_specs=[pl.BlockSpec(memory_space=pl.ANY)],
        out_specs=[pl.BlockSpec(memory_space=pltpu.VMEM)] * 2,
        scratch_shapes=[
            pltpu.SemaphoreType.DMA((12,)),
            pltpu.SemaphoreType.DMA((12,)),
        ],
        compiler_params=pltpu.CompilerParams(collective_id=0, has_side_effects=True),
    )(frames)


def rounded(value):
    return value.astype(jnp.bfloat16)


def predict_kernel(
    ha_count,
    wa_count,
    win0,
    win1,
    conv_first,
    conv_second,
    norm_attn,
    qkv_weight,
    out_weight,
    norm_mlp,
    mlp_in,
    mlp_out,
    target,
    predicted,
    loss,
    bias,
    blended,
    patches,
    hidden,
    patches_hidden,
    encoded,
    paired,
):
    row_count = win0.shape[0] - 2 * RIMS[0]
    width = win0.shape[1]
    col_count = width - 2 * SIDE
    channels = win0.shape[2]
    here_t, here_a, here_w = (lax.axis_index(n) for n in ("tm", "ha", "wa"))
    first_row = (here_a * 2 + here_t) * row_count
    first_col = here_w * col_count
    image_rows = ha_count * 2 * row_count
    image_cols = wa_count * col_count

    def in_image(shape, row_start, col_start):
        row = lax.broadcasted_iota(jnp.int32, shape, 0) + row_start
        col = lax.broadcasted_iota(jnp.int32, shape, 1) + col_start
        return (row >= 0) & (row < image_rows) & (col >= 0) & (col < image_cols)

    krows, kcols = QROWS + 2 * RADIUS, QCOLS + 16
    queries_n, keys_n = QROWS * QCOLS, krows * kcols
    q_at = lax.broadcasted_iota(jnp.int32, (queries_n, keys_n), 0)
    k_at = lax.broadcasted_iota(jnp.int32, (queries_n, keys_n), 1)
    d_row = k_at // kcols - q_at // QCOLS
    d_col = k_at % kcols - q_at % QCOLS - (8 - RADIUS)
    near = (d_row >= 0) & (d_row <= 2 * RADIUS) & (d_col >= 0) & (d_col <= 2 * RADIUS)
    bias[...] = jnp.where(near, 0.0, -1e30)
    scale = channels ** (-0.5) * 1.4426950408889634

    @pl.loop(0, win0.shape[0] // QROWS)
    def _(step):
        top_row = step * QROWS
        for start in range(8, width - 8, QCOLS):
            query = win0[pl.ds(top_row, QROWS), start : start + QCOLS].reshape(
                queries_n, channels
            )
            keys = win1[pl.ds(top_row, krows), start - 8 : start + QCOLS + 8].reshape(
                keys_n, channels
            )
            scores = lax.dot_general(
                query, keys, (((1,), (1,)), ((), ())), preferred_element_type=jnp.float32
            )
            scores = scores * scale + bias[...]
            expo = jnp.exp2(scores - jnp.max(scores, axis=-1, keepdims=True))
            total = jnp.sum(expo, axis=-1, keepdims=True)
            found = jnp.dot(rounded(expo), keys, preferred_element_type=jnp.float32) / total
            mixed = rounded(query.astype(jnp.float32) + found).astype(jnp.float32)
            mixed = mixed.reshape(QROWS, QCOLS, channels)
            keep = in_image(
                mixed.shape, first_row - RIMS[0] + top_row, first_col - SIDE + start
            )
            blended[pl.ds(top_row, QROWS), start : start + QCOLS] = jnp.where(keep, mixed, 0.0)

    for frame in range(2):
        if frame == 1:
            gap = RIMS[1] - RIMS[0]
            blended[...] = win1[gap : gap + win0.shape[0]].astype(jnp.float32)
        for tap in range(3):
            patches[:, :, tap * channels : (tap + 1) * channels] = rounded(
                blended[:, 7 + tap : width - 9 + tap]
            )

        @pl.loop(0, (row_count + 2) // 6)
        def _(step):
            at = step * 6
            lhs = jnp.concatenate([patches[pl.ds(at + i, 6)] for i in range(3)], axis=-1)
            shape = (6, width - 16, channels)
            out = jnp.dot(
                lhs.reshape(-1, 9 * channels), conv_first[...], preferred_element_type=jnp.float32
            )
            out = rounded(jax.nn.gelu(out)).astype(jnp.float32).reshape(shape)
            keep = in_image(shape, first_row - 1 + at, first_col - 8)
            hidden[pl.ds(at, 6)] = jnp.where(keep, out, 0.0)

        for tap in range(3):
            patches_hidden[:, :, tap * channels : (tap + 1) * channels] = rounded(
                hidden[:, 7 + tap : 7 + tap + col_count]
            )

        @pl.loop(0, row_count // 8)
        def _(step):
            at = step * 8
            lhs = jnp.concatenate([patches_hidden[pl.ds(at + i, 8)] for i in range(3)], axis=-1)
            out = jnp.dot(
                lhs.reshape(-1, 9 * channels), conv_second[...], preferred_element_type=jnp.float32
            )
            base = blended[pl.ds(at + 2, 8), SIDE : SIDE + col_count].reshape(out.shape)
            encoded[frame, pl.ds(at * col_count, 8 * col_count)] = rounded(base + out).astype(
                jnp.float32
            )

    depth = channels // HEADS
    lane_in = lax.broadcasted_iota(jnp.int32, (2 * channels, channels), 0) % channels
    lane_out = lax.broadcasted_iota(jnp.int32, (2 * channels, channels), 1)
    head_sum = rounded(jnp.where(lane_in // depth == lane_out // depth, 1.0, 0.0))
    chunk = 256

    def unit(value, gain):
        mean = jnp.mean(value * value, axis=-1, keepdims=True)
        return rounded(value * lax.rsqrt(mean + EPSILON) * gain[...])

    def dot(left, right):
        return jnp.dot(left, right, preferred_element_type=jnp.float32)

    @pl.loop(0, row_count * col_count // chunk, init_carry=jnp.zeros((8, channels), jnp.float32))
    def errors(step, carry):
        at = pl.multiple_of(step * chunk, chunk)
        series = jnp.concatenate([encoded[0, pl.ds(at, chunk)], encoded[1, pl.ds(at, chunk)]])
        projected = rounded(dot(unit(series, norm_attn), qkv_weight[...])).astype(jnp.float32)
        query = projected[chunk:, :channels]
        keys = projected[:, channels : 2 * channels]
        values = projected[:, 2 * channels :]
        product = query * (keys[chunk:] - keys[:chunk])
        high = rounded(product)
        low = rounded(product - high.astype(jnp.float32))
        gap = dot(jnp.concatenate([high, low], axis=-1), head_sum) * depth ** (-0.5)
        half = 0.5 * jnp.tanh(0.5 * gap)
        weight_now = rounded(0.5 + half).astype(jnp.float32)
        weight_past = rounded(0.5 - half).astype(jnp.float32)
        attended = weight_past * values[:chunk] + weight_now * values[chunk:]
        attended = rounded(jnp.concatenate([values[:chunk], attended]))
        resid = series + dot(attended, out_weight[...])
        inner = rounded(jax.nn.gelu(dot(unit(resid, norm_mlp), mlp_in[...])))
        output = resid + dot(inner, mlp_out[...])
        paired[pl.ds(0, chunk, stride=2)] = output[:chunk]
        paired[pl.ds(1, chunk, stride=2)] = output[chunk:]
        final = rounded(paired[...])
        both = pl.ds(pl.multiple_of(2 * at, 2 * chunk), 2 * chunk)
        predicted[both] = final
        error = final.astype(jnp.float32) - target[both].astype(jnp.float32)
        return carry + jnp.sum((error * error).reshape(-1, 8, channels), axis=0)

    loss[...] = errors


def predict(win0, win1, weights, target):
    row_count = win0.shape[0] - 2 * RIMS[0]
    width, channels = win0.shape[1:]
    col_count = width - 2 * SIDE
    ha_count, wa_count = lax.axis_size("ha"), lax.axis_size("wa")

    def kernel(*refs):
        predict_kernel(ha_count, wa_count, *refs)

    tokens = 2 * row_count * col_count
    operands = (win0, win1, *weights, target)
    return pl.pallas_call(
        kernel,
        out_shape=[
            jax.ShapeDtypeStruct((tokens, channels), jnp.bfloat16),
            jax.ShapeDtypeStruct((8, channels), jnp.float32),
        ],
        in_specs=[pl.BlockSpec(memory_space=pltpu.VMEM)] * len(operands),
        out_specs=[pl.BlockSpec(memory_space=pltpu.VMEM)] * 2,
        scratch_shapes=[
            pltpu.VMEM((QROWS * QCOLS, (QROWS + 2 * RADIUS) * (QCOLS + 16)), jnp.float32),
            pltpu.VMEM((row_count + 4, width, channels), jnp.float32),
            pltpu.VMEM((row_count + 4, width - 16, 3 * channels), jnp.bfloat16),
            pltpu.VMEM((row_count + 2, width - 16, channels), jnp.float32),
            pltpu.VMEM((row_count + 2, col_count, 3 * channels), jnp.bfloat16),
            pltpu.VMEM((2, row_count * col_count, channels), jnp.float32),
            pltpu.VMEM((512, channels), jnp.float32),
        ],
        compiler_params=pltpu.CompilerParams(vmem_limit_bytes=60 * 1024 * 1024),
    )(*operands)


def total_kernel(
    wa_count, ha_count, near_count, scale, errors, total, near, part, far, near_sems, far_sems
):
    here_t, here_a, here_w = (lax.axis_index(n) for n in ("tm", "ha", "wa"))
    here = here_t * wa_count + here_w

    def near_peer(step):
        slot = lax.rem(here + step, near_count)
        return slot, (slot // wa_count, here_a, lax.rem(slot, wa_count))

    def far_peer(step):
        slot = lax.rem(here_a + step, ha_count)
        return slot, (here_t, slot, here_w)

    barrier = pltpu.get_barrier_semaphore()
    groups = ((near_peer, near_count), (far_peer, ha_count))
    for peer, count in groups:
        for step in range(1, count):
            pl.semaphore_signal(
                barrier,
                inc=1,
                device_id=peer(step)[1],
                device_id_type=pl.DeviceIdType.MESH,
            )
    pl.semaphore_wait(barrier, near_count + ha_count - 2)

    def exchange(source, slots, sems, peer, count, own):
        def copy(step, slot, device):
            return pltpu.make_async_remote_copy(
                src_ref=source,
                dst_ref=slots.at[slot],
                send_sem=sems.at[0, step],
                recv_sem=sems.at[1, slot],
                device_id=device,
                device_id_type=pl.DeviceIdType.MESH,
            )

        for step in range(1, count):
            copy(step, own, peer(step)[1]).start()
        slots[own] = source[...]
        for step in range(1, count):
            slot, device = peer(step)
            copy(step, slot, device).wait_recv()
        for step in range(1, count):
            copy(step, own, peer(step)[1]).wait_send()
        summed = slots[0]
        for slot in range(1, count):
            summed = summed + slots[slot]
        return summed

    part[...] = exchange(errors, near, near_sems, near_peer, near_count, here)
    summed = exchange(part, far, far_sems, far_peer, ha_count, here_a)
    total[0, 0] = jnp.sum(summed) * scale


def total_error(errors, entries):
    ha_count, wa_count = lax.axis_size("ha"), lax.axis_size("wa")
    near_count = lax.axis_size("tm") * wa_count

    def kernel(*refs):
        total_kernel(wa_count, ha_count, near_count, 1.0 / entries, *refs)

    return pl.pallas_call(
        kernel,
        out_shape=jax.ShapeDtypeStruct((1, 1), jnp.float32),
        in_specs=[pl.BlockSpec(memory_space=pltpu.VMEM)],
        out_specs=pl.BlockSpec(memory_space=pltpu.SMEM),
        scratch_shapes=[
            pltpu.VMEM((near_count, *errors.shape), jnp.float32),
            pltpu.VMEM(errors.shape, jnp.float32),
            pltpu.VMEM((ha_count, *errors.shape), jnp.float32),
            pltpu.SemaphoreType.DMA((2, near_count)),
            pltpu.SemaphoreType.DMA((2, ha_count)),
        ],
        compiler_params=pltpu.CompilerParams(collective_id=1, has_side_effects=True),
    )(errors)


def pair_shards(
    frames,
    conv_first,
    conv_second,
    norm_attn,
    qkv_weight,
    out_weight,
    norm_mlp,
    mlp_in,
    mlp_out,
    target,
):
    channels = frames.shape[3]
    win0, win1 = gather_windows(frames)
    weights = (
        conv_first.reshape(-1, channels),
        conv_second.reshape(-1, channels),
        norm_attn.reshape(1, channels),
        qkv_weight,
        out_weight,
        norm_mlp.reshape(1, channels),
        mlp_in,
        mlp_out,
    )
    predicted, errors = predict(win0, win1, weights, target.reshape(-1, channels))
    entries = target.size * lax.axis_size("tm") * lax.axis_size("ha") * lax.axis_size("wa")
    return (predicted.reshape(target.shape), total_error(errors, entries).reshape(()))


def solution(mesh):
    in_specs = (
        P("tm", "ha", "wa", None),
        P(),
        P(),
        P(),
        P(),
        P(),
        P(),
        P(),
        P(),
        P(("ha", "tm"), "wa", None, None),
    )
    out_specs = (P(("ha", "tm"), "wa", None, None), P())
    body = pair_shards if mesh.shape["tm"] == 2 else shards
    return jax.shard_map(body, mesh=mesh, in_specs=in_specs, out_specs=out_specs, check_vma=False)
```

```python
import jax
import jax.numpy as jnp
from jax import lax
from jax.experimental import pallas as pl
from jax.experimental.pallas import tpu as pltpu
from jax.sharding import PartitionSpec as P

HEADS = 4
RADIUS = 4


EPSILON = 1e-06


def shifted(value, axis, steps):
    count = lax.axis_size(axis)
    initial, last = (max(0, -steps), min(count, count - steps))
    return lax.ppermute(value, axis, [(source, source + steps) for source in range(initial, last)])


def with_halo(block, sides, width):
    for axis, dim in sides:
        count = lax.axis_size(axis)
        forward = [(i, i + 1) for i in range(count - 1)]
        backward = [(target, source) for source, target in forward]
        low = lax.ppermute(
            lax.slice_in_dim(block, block.shape[dim] - width, None, axis=dim), axis, forward
        )
        high = lax.ppermute(lax.slice_in_dim(block, 0, width, axis=dim), axis, backward)
        block = jnp.concatenate([low, block, high], axis=dim)
    return block


def convolve(padded, kernel, row_count, col_count):
    nframes = padded.shape[0]
    summed = jnp.zeros((nframes * row_count * col_count, kernel.shape[3]), jnp.float32)
    for tap_row in range(3):
        for tap_col in range(3):
            patch = padded[:, tap_row : tap_row + row_count, tap_col : tap_col + col_count]
            summed = summed + jnp.dot(
                patch.reshape(-1, patch.shape[3]),
                kernel[tap_row, tap_col],
                preferred_element_type=jnp.float32,
            )
    return summed.reshape(nframes, row_count, col_count, -1)


def correlate(current, windowed):
    nframes, tile_rows, tile_cols, channels = current.shape
    span = 2 * RADIUS + 1
    reach = tile_cols + 2 * RADIUS
    col_here = jnp.arange(tile_cols)[:, None, None]
    col_there = jnp.arange(reach)[None, :, None]
    offsets = jnp.arange(span)[None, None, :]
    band = col_there == col_here + offsets
    band_f32 = band.astype(jnp.float32)
    band_bf16 = band.astype(jnp.bfloat16)
    pieces = []
    for shift_row in range(span):
        rows_window = windowed[:, shift_row : shift_row + tile_rows]
        banded = jnp.einsum(
            "fhic,fhjc->fhij", current, rows_window, preferred_element_type=jnp.float32
        )
        pieces.append(
            jnp.einsum("fhij,ijb->fhib", banded, band_f32, precision=lax.Precision.HIGHEST)
        )
    scores = jnp.concatenate(pieces, axis=-1) * channels ** (-0.5)
    top = jnp.max(scores, axis=-1, keepdims=True)
    expo = jnp.exp(scores - top)
    probs = (expo / jnp.sum(expo, axis=-1, keepdims=True)).astype(jnp.bfloat16)
    gathered = jnp.zeros(current.shape, jnp.float32)
    for shift_row in range(span):
        rows_window = windowed[:, shift_row : shift_row + tile_rows]
        chosen = probs[..., shift_row * span : (shift_row + 1) * span]
        spread = jnp.einsum(
            "fhib,ijb->fhij", chosen, band_bf16, preferred_element_type=jnp.float32
        ).astype(jnp.bfloat16)
        gathered = gathered + jnp.einsum(
            "fhij,fhjc->fhic", spread, rows_window, preferred_element_type=jnp.float32
        )
    return (current.astype(jnp.float32) + gathered).astype(jnp.bfloat16)


def project(series, norm_attn, qkv_weight):
    npos, nframes, channels = series.shape
    base = series.astype(jnp.float32)
    normed = (
        base * lax.rsqrt(jnp.mean(base * base, axis=-1, keepdims=True) + EPSILON) * norm_attn
    ).astype(jnp.bfloat16)
    projected = jnp.dot(
        normed.reshape(-1, channels), qkv_weight, preferred_element_type=jnp.float32
    ).astype(jnp.bfloat16)
    projected = projected.reshape(npos, nframes, 3 * channels)
    return (
        projected[..., :channels],
        projected[..., channels : 2 * channels],
        projected[..., 2 * channels :],
    )


def attend(queries, key_rows, value_rows, query_ids, key_ids):
    npos, query_count, channels = queries.shape
    key_count = key_rows.shape[1]
    depth = channels // HEADS
    query_heads = queries.reshape(npos, query_count, HEADS, depth)
    key_heads = key_rows.reshape(npos, key_count, HEADS, depth)
    value_heads = value_rows.reshape(npos, key_count, HEADS, depth)
    scores = jnp.einsum(
        "pqhd,pkhd->phqk", query_heads, key_heads, preferred_element_type=jnp.float32
    ) * depth ** (-0.5)
    allowed = key_ids[None, :] <= query_ids[:, None]
    scores = jnp.where(allowed, scores, -1e30)
    top = jnp.max(scores, axis=-1, keepdims=True)
    expo = jnp.exp(scores - top)
    weights = (expo / jnp.sum(expo, axis=-1, keepdims=True)).astype(jnp.bfloat16)
    attended = jnp.einsum(
        "phqk,pkhd->pqhd", weights, value_heads, preferred_element_type=jnp.float32
    )
    return attended.reshape(npos, query_count, channels).astype(jnp.bfloat16)


def finish(series, attended, out_weight, norm_mlp, mlp_in, mlp_out):
    npos, nframes, channels = series.shape
    resid = series.astype(jnp.float32) + jnp.dot(
        attended.reshape(-1, channels), out_weight, preferred_element_type=jnp.float32
    ).reshape(npos, nframes, channels)
    mlp_input = (
        resid * lax.rsqrt(jnp.mean(resid * resid, axis=-1, keepdims=True) + EPSILON) * norm_mlp
    ).astype(jnp.bfloat16)
    mlp_hidden = jax.nn.gelu(
        jnp.dot(mlp_input.reshape(-1, channels), mlp_in, preferred_element_type=jnp.float32)
    ).astype(jnp.bfloat16)
    output = resid + jnp.dot(mlp_hidden, mlp_out, preferred_element_type=jnp.float32).reshape(
        npos, nframes, channels
    )
    return output.astype(jnp.bfloat16)


def shards(
    frames,
    conv_first,
    conv_second,
    norm_attn,
    qkv_weight,
    out_weight,
    norm_mlp,
    mlp_in,
    mlp_out,
    target,
):
    frame_count, tile_rows, tile_cols, channels = frames.shape
    arrival = shifted(frames, "tm", -1)
    following = jnp.concatenate([frames[1:], arrival], axis=0)
    windowed = with_halo(following, (("ha", 1), ("wa", 2)), RADIUS)
    blended = correlate(frames, windowed)
    padded_first = with_halo(blended, (("ha", 1), ("wa", 2)), 1)
    hidden_map = jax.nn.gelu(convolve(padded_first, conv_first, tile_rows, tile_cols)).astype(
        jnp.bfloat16
    )
    hidden_map = with_halo(hidden_map, (("ha", 1), ("wa", 2)), 1)
    encoded = (
        blended.astype(jnp.float32) + convolve(hidden_map, conv_second, tile_rows, tile_cols)
    ).astype(jnp.bfloat16)
    series = jnp.transpose(
        lax.all_to_all(encoded, "tm", split_axis=1, concat_axis=0, tiled=True), (1, 2, 0, 3)
    )
    layout = series.shape
    tokens_flat = series.reshape(-1, layout[2], layout[3])
    frame_ids = jnp.arange(layout[2])
    queries, key_rows, value_rows = project(tokens_flat, norm_attn, qkv_weight)
    attended = attend(queries, key_rows, value_rows, frame_ids, frame_ids)
    predicted = finish(tokens_flat, attended, out_weight, norm_mlp, mlp_in, mlp_out).reshape(layout)
    errors = predicted.astype(jnp.float32) - target.astype(jnp.float32)
    summed = lax.psum(jnp.sum(errors * errors), ("tm", "ha", "wa"))
    entries = predicted.size * lax.axis_size("tm") * lax.axis_size("ha") * lax.axis_size("wa")
    return (predicted, summed / entries)


RIMS = (2, RADIUS + 2)
SIDE = 16
QROWS = 20
QCOLS = 16


def window_parts(frame, place, tile_rows, tile_cols):
    rim = RIMS[frame]
    main = tile_rows // 2 + rim
    if place == 0:
        rows = [(0, main, rim, 0), (tile_rows - rim, rim, 0, -1)]
    else:
        rows = [(tile_rows - main, main, 0, 0), (0, rim, main, 1)]
    cols = [
        (0, tile_cols, SIDE, 0),
        (tile_cols - SIDE, SIDE, 0, -1),
        (0, SIDE, SIDE + tile_cols, 1),
    ]
    return [(row, col) for row in rows for col in cols]


def gather_kernel(
    ha_count, wa_count, frames_ref, win0, win1, send_sem, recv_sem
):
    wins = (win0, win1)
    _, tile_rows, tile_cols, _ = frames_ref.shape
    here_t, here_a, here_w = (lax.axis_index(n) for n in ("tm", "ha", "wa"))
    barrier = pltpu.get_barrier_semaphore()

    def inside(a, w):
        return (a >= 0) & (a < ha_count) & (w >= 0) & (w < wa_count)

    def device(t, a, w):
        wrapped = (lax.rem(a + ha_count, ha_count), lax.rem(w + wa_count, wa_count))
        return (jnp.int32(t), *wrapped)

    def branch(mine):
        other = 1 - mine
        expected = jnp.int32(0)
        for frame in range(2):
            for row, col in window_parts(frame, mine, tile_rows, tile_cols):
                a, w = here_a + row[3], here_w + col[3]
                if frame == mine and row[3] == 0 and col[3] == 0:
                    continue

                @pl.when(inside(a, w))
                def _():
                    pl.semaphore_signal(
                        barrier,
                        inc=1,
                        device_id=device(frame, a, w),
                        device_id_type=pl.DeviceIdType.MESH,
                    )

        sends = []
        for place in range(2):
            for slot, (row, col) in enumerate(
                window_parts(mine, place, tile_rows, tile_cols)
            ):
                a, w = here_a - row[3], here_w - col[3]
                local = place == mine and row[3] == 0 and col[3] == 0
                source = frames_ref.at[0, pl.ds(row[0], row[1]), pl.ds(col[0], col[1])]
                target = wins[mine].at[pl.ds(row[2], row[1]), pl.ds(col[2], col[1])]
                if local:
                    own = pltpu.make_async_copy(source, target, recv_sem.at[mine * 6 + slot])
                    continue
                expected = expected + inside(a, w).astype(jnp.int32)
                sends.append(
                    (
                        inside(a, w),
                        pltpu.make_async_remote_copy(
                            src_ref=source,
                            dst_ref=target,
                            send_sem=send_sem.at[place * 6 + slot],
                            recv_sem=recv_sem.at[mine * 6 + slot],
                            device_id=device(place, a, w),
                            device_id_type=pl.DeviceIdType.MESH,
                        ),
                    )
                )
        own.start()
        arrivals = []
        for frame in range(2):
            for slot, (row, col) in enumerate(
                window_parts(frame, mine, tile_rows, tile_cols)
            ):
                a, w = here_a + row[3], here_w + col[3]
                if frame == mine and row[3] == 0 and col[3] == 0:
                    continue
                target = wins[frame].at[pl.ds(row[2], row[1]), pl.ds(col[2], col[1])]

                def clear(target=target):
                    target[...] = jnp.zeros(target.shape, target.dtype)

                arrival = pltpu.make_async_remote_copy(
                    src_ref=target,
                    dst_ref=target,
                    send_sem=send_sem.at[frame * 6 + slot],
                    recv_sem=recv_sem.at[frame * 6 + slot],
                    device_id=device(other, here_a, here_w),
                    device_id_type=pl.DeviceIdType.MESH,
                )
                arrivals.append((inside(a, w), arrival))
                pl.when(jnp.logical_not(inside(a, w)))(clear)
        pl.semaphore_wait(barrier, expected)
        for exists, copy in sends:
            pl.when(exists)(copy.start)
        own.wait()
        for exists, arrival in arrivals:
            pl.when(exists)(arrival.wait_recv)
        for exists, copy in sends:
            pl.when(exists)(copy.wait_send)

    pl.when(here_t == 0)(lambda: branch(0))
    pl.when(here_t == 1)(lambda: branch(1))


def gather_windows(frames):
    _, tile_rows, tile_cols, channels = frames.shape
    shapes = [
        jax.ShapeDtypeStruct(
            (tile_rows // 2 + 2 * rim, tile_cols + 2 * SIDE, channels), frames.dtype
        )
        for rim in RIMS
    ]
    ha_count, wa_count = lax.axis_size("ha"), lax.axis_size("wa")

    def kernel(*refs):
        gather_kernel(ha_count, wa_count, *refs)

    return pl.pallas_call(
        kernel,
        out_shape=shapes,
        in_specs=[pl.BlockSpec(memory_space=pl.ANY)],
        out_specs=[pl.BlockSpec(memory_space=pltpu.VMEM)] * 2,
        scratch_shapes=[
            pltpu.SemaphoreType.DMA((12,)),
            pltpu.SemaphoreType.DMA((12,)),
        ],
        compiler_params=pltpu.CompilerParams(collective_id=0, has_side_effects=True),
    )(frames)


def rounded(value):
    return value.astype(jnp.bfloat16)


def predict_kernel(
    ha_count,
    wa_count,
    win0,
    win1,
    conv_first,
    conv_second,
    norm_attn,
    qkv_weight,
    out_weight,
    norm_mlp,
    mlp_in,
    mlp_out,
    target,
    predicted,
    loss,
    bias,
    blended,
    patches,
    hidden,
    patches_hidden,
    encoded,
    paired,
):
    row_count = win0.shape[0] - 2 * RIMS[0]
    width = win0.shape[1]
    col_count = width - 2 * SIDE
    channels = win0.shape[2]
    here_t, here_a, here_w = (lax.axis_index(n) for n in ("tm", "ha", "wa"))
    first_row = (here_a * 2 + here_t) * row_count
    first_col = here_w * col_count
    image_rows = ha_count * 2 * row_count
    image_cols = wa_count * col_count

    def in_image(shape, row_start, col_start):
        row = lax.broadcasted_iota(jnp.int32, shape, 0) + row_start
        col = lax.broadcasted_iota(jnp.int32, shape, 1) + col_start
        return (row >= 0) & (row < image_rows) & (col >= 0) & (col < image_cols)

    krows, kcols = QROWS + 2 * RADIUS, QCOLS + 16
    queries_n, keys_n = QROWS * QCOLS, krows * kcols
    q_at = lax.broadcasted_iota(jnp.int32, (queries_n, keys_n), 0)
    k_at = lax.broadcasted_iota(jnp.int32, (queries_n, keys_n), 1)
    d_row = k_at // kcols - q_at // QCOLS
    d_col = k_at % kcols - q_at % QCOLS - (8 - RADIUS)
    near = (d_row >= 0) & (d_row <= 2 * RADIUS) & (d_col >= 0) & (d_col <= 2 * RADIUS)
    bias[...] = jnp.where(near, 0.0, -1e30)
    scale = channels ** (-0.5) * 1.4426950408889634

    @pl.loop(0, win0.shape[0] // QROWS)
    def _(step):
        top_row = step * QROWS
        for start in range(8, width - 8, QCOLS):
            query = win0[pl.ds(top_row, QROWS), start : start + QCOLS].reshape(
                queries_n, channels
            )
            keys = win1[pl.ds(top_row, krows), start - 8 : start + QCOLS + 8].reshape(
                keys_n, channels
            )
            scores = lax.dot_general(
                query, keys, (((1,), (1,)), ((), ())), preferred_element_type=jnp.float32
            )
            scores = scores * scale + bias[...]
            expo = jnp.exp2(scores - jnp.max(scores, axis=-1, keepdims=True))
            total = jnp.sum(expo, axis=-1, keepdims=True)
            found = jnp.dot(rounded(expo), keys, preferred_element_type=jnp.float32) / total
            mixed = rounded(query.astype(jnp.float32) + found).astype(jnp.float32)
            mixed = mixed.reshape(QROWS, QCOLS, channels)
            keep = in_image(
                mixed.shape, first_row - RIMS[0] + top_row, first_col - SIDE + start
            )
            blended[pl.ds(top_row, QROWS), start : start + QCOLS] = jnp.where(keep, mixed, 0.0)

    for frame in range(2):
        if frame == 1:
            gap = RIMS[1] - RIMS[0]
            blended[...] = win1[gap : gap + win0.shape[0]].astype(jnp.float32)
        for tap in range(3):
            patches[:, :, tap * channels : (tap + 1) * channels] = rounded(
                blended[:, 7 + tap : width - 9 + tap]
            )

        @pl.loop(0, (row_count + 2) // 9)
        def _(step):
            at = step * 9
            lhs = jnp.concatenate([patches[pl.ds(at + i, 9)] for i in range(3)], axis=-1)
            shape = (9, width - 16, channels)
            out = jnp.dot(
                lhs.reshape(-1, 9 * channels), conv_first[...], preferred_element_type=jnp.float32
            )
            out = rounded(jax.nn.gelu(out)).astype(jnp.float32).reshape(shape)
            keep = in_image(shape, first_row - 1 + at, first_col - 8)
            hidden[pl.ds(at, 9)] = jnp.where(keep, out, 0.0)

        for tap in range(3):
            patches_hidden[:, :, tap * channels : (tap + 1) * channels] = rounded(
                hidden[:, 7 + tap : 7 + tap + col_count]
            )

        @pl.loop(0, row_count // 8)
        def _(step):
            at = step * 8
            lhs = jnp.concatenate([patches_hidden[pl.ds(at + i, 8)] for i in range(3)], axis=-1)
            out = jnp.dot(
                lhs.reshape(-1, 9 * channels), conv_second[...], preferred_element_type=jnp.float32
            )
            base = blended[pl.ds(at + 2, 8), SIDE : SIDE + col_count].reshape(out.shape)
            encoded[frame, pl.ds(at * col_count, 8 * col_count)] = rounded(base + out).astype(
                jnp.float32
            )

    depth = channels // HEADS
    lane_in = lax.broadcasted_iota(jnp.int32, (2 * channels, channels), 0) % channels
    lane_out = lax.broadcasted_iota(jnp.int32, (2 * channels, channels), 1)
    head_sum = rounded(jnp.where(lane_in // depth == lane_out // depth, 1.0, 0.0))
    chunk = 1024

    def unit(value, gain):
        mean = jnp.mean(value * value, axis=-1, keepdims=True)
        return rounded(value * lax.rsqrt(mean + EPSILON) * gain[...])

    def dot(left, right):
        return jnp.dot(left, right, preferred_element_type=jnp.float32)

    @pl.loop(0, row_count * col_count // chunk, init_carry=jnp.zeros((8, channels), jnp.float32))
    def errors(step, carry):
        at = pl.multiple_of(step * chunk, chunk)
        series = jnp.concatenate([encoded[0, pl.ds(at, chunk)], encoded[1, pl.ds(at, chunk)]])
        projected = rounded(dot(unit(series, norm_attn), qkv_weight[...])).astype(jnp.float32)
        query = projected[chunk:, :channels]
        keys = projected[:, channels : 2 * channels]
        values = projected[:, 2 * channels :]
        product = query * (keys[chunk:] - keys[:chunk])
        high = rounded(product)
        low = rounded(product - high.astype(jnp.float32))
        gap = dot(jnp.concatenate([high, low], axis=-1), head_sum) * depth ** (-0.5)
        half = 0.5 * jnp.tanh(0.5 * gap)
        weight_now = rounded(0.5 + half).astype(jnp.float32)
        weight_past = rounded(0.5 - half).astype(jnp.float32)
        attended = weight_past * values[:chunk] + weight_now * values[chunk:]
        attended = rounded(jnp.concatenate([values[:chunk], attended]))
        resid = series + dot(attended, out_weight[...])
        inner = rounded(jax.nn.gelu(dot(unit(resid, norm_mlp), mlp_in[...])))
        output = resid + dot(inner, mlp_out[...])
        paired[pl.ds(0, chunk, stride=2)] = output[:chunk]
        paired[pl.ds(1, chunk, stride=2)] = output[chunk:]
        final = rounded(paired[...])
        both = pl.ds(pl.multiple_of(2 * at, 2 * chunk), 2 * chunk)
        predicted[both] = final
        error = final.astype(jnp.float32) - target[both].astype(jnp.float32)
        return carry + jnp.sum((error * error).reshape(-1, 8, channels), axis=0)

    loss[...] = errors


def predict(win0, win1, weights, target):
    row_count = win0.shape[0] - 2 * RIMS[0]
    width, channels = win0.shape[1:]
    col_count = width - 2 * SIDE
    ha_count, wa_count = lax.axis_size("ha"), lax.axis_size("wa")

    def kernel(*refs):
        predict_kernel(ha_count, wa_count, *refs)

    tokens = 2 * row_count * col_count
    operands = (win0, win1, *weights, target)
    return pl.pallas_call(
        kernel,
        out_shape=[
            jax.ShapeDtypeStruct((tokens, channels), jnp.bfloat16),
            jax.ShapeDtypeStruct((8, channels), jnp.float32),
        ],
        in_specs=[pl.BlockSpec(memory_space=pltpu.VMEM)] * len(operands),
        out_specs=[pl.BlockSpec(memory_space=pltpu.VMEM)] * 2,
        scratch_shapes=[
            pltpu.VMEM((QROWS * QCOLS, (QROWS + 2 * RADIUS) * (QCOLS + 16)), jnp.float32),
            pltpu.VMEM((row_count + 4, width, channels), jnp.float32),
            pltpu.VMEM((row_count + 4, width - 16, 3 * channels), jnp.bfloat16),
            pltpu.VMEM((row_count + 2, width - 16, channels), jnp.float32),
            pltpu.VMEM((row_count + 2, col_count, 3 * channels), jnp.bfloat16),
            pltpu.VMEM((2, row_count * col_count, channels), jnp.float32),
            pltpu.VMEM((2048, channels), jnp.float32),
        ],
        compiler_params=pltpu.CompilerParams(vmem_limit_bytes=60 * 1024 * 1024),
    )(*operands)


def total_kernel(
    wa_count, ha_count, near_count, scale, errors, total, near, part, far, near_sems, far_sems
):
    here_t, here_a, here_w = (lax.axis_index(n) for n in ("tm", "ha", "wa"))
    here = here_t * wa_count + here_w

    def near_peer(step):
        slot = lax.rem(here + step, near_count)
        return slot, (slot // wa_count, here_a, lax.rem(slot, wa_count))

    def far_peer(step):
        slot = lax.rem(here_a + step, ha_count)
        return slot, (here_t, slot, here_w)

    barrier = pltpu.get_barrier_semaphore()
    groups = ((near_peer, near_count), (far_peer, ha_count))
    for peer, count in groups:
        for step in range(1, count):
            pl.semaphore_signal(
                barrier,
                inc=1,
                device_id=peer(step)[1],
                device_id_type=pl.DeviceIdType.MESH,
            )
    pl.semaphore_wait(barrier, near_count + ha_count - 2)

    def exchange(source, slots, sems, peer, count, own):
        def copy(step, slot, device):
            return pltpu.make_async_remote_copy(
                src_ref=source,
                dst_ref=slots.at[slot],
                send_sem=sems.at[0, step],
                recv_sem=sems.at[1, slot],
                device_id=device,
                device_id_type=pl.DeviceIdType.MESH,
            )

        for step in range(1, count):
            copy(step, own, peer(step)[1]).start()
        slots[own] = source[...]
        for step in range(1, count):
            slot, device = peer(step)
            copy(step, slot, device).wait_recv()
        for step in range(1, count):
            copy(step, own, peer(step)[1]).wait_send()
        summed = slots[0]
        for slot in range(1, count):
            summed = summed + slots[slot]
        return summed

    part[...] = exchange(errors, near, near_sems, near_peer, near_count, here)
    summed = exchange(part, far, far_sems, far_peer, ha_count, here_a)
    total[0, 0] = jnp.sum(summed) * scale


def total_error(errors, entries):
    ha_count, wa_count = lax.axis_size("ha"), lax.axis_size("wa")
    near_count = lax.axis_size("tm") * wa_count

    def kernel(*refs):
        total_kernel(wa_count, ha_count, near_count, 1.0 / entries, *refs)

    return pl.pallas_call(
        kernel,
        out_shape=jax.ShapeDtypeStruct((1, 1), jnp.float32),
        in_specs=[pl.BlockSpec(memory_space=pltpu.VMEM)],
        out_specs=pl.BlockSpec(memory_space=pltpu.SMEM),
        scratch_shapes=[
            pltpu.VMEM((near_count, *errors.shape), jnp.float32),
            pltpu.VMEM(errors.shape, jnp.float32),
            pltpu.VMEM((ha_count, *errors.shape), jnp.float32),
            pltpu.SemaphoreType.DMA((2, near_count)),
            pltpu.SemaphoreType.DMA((2, ha_count)),
        ],
        compiler_params=pltpu.CompilerParams(collective_id=1, has_side_effects=True),
    )(errors)


def pair_shards(
    frames,
    conv_first,
    conv_second,
    norm_attn,
    qkv_weight,
    out_weight,
    norm_mlp,
    mlp_in,
    mlp_out,
    target,
):
    channels = frames.shape[3]
    win0, win1 = gather_windows(frames)
    weights = (
        conv_first.reshape(-1, channels),
        conv_second.reshape(-1, channels),
        norm_attn.reshape(1, channels),
        qkv_weight,
        out_weight,
        norm_mlp.reshape(1, channels),
        mlp_in,
        mlp_out,
    )
    predicted, errors = predict(win0, win1, weights, target.reshape(-1, channels))
    entries = target.size * lax.axis_size("tm") * lax.axis_size("ha") * lax.axis_size("wa")
    return (predicted.reshape(target.shape), total_error(errors, entries).reshape(()))


def solution(mesh):
    in_specs = (
        P("tm", "ha", "wa", None),
        P(),
        P(),
        P(),
        P(),
        P(),
        P(),
        P(),
        P(),
        P(("ha", "tm"), "wa", None, None),
    )
    out_specs = (P(("ha", "tm"), "wa", None, None), P())
    body = pair_shards if mesh.shape["tm"] == 2 else shards
    return jax.shard_map(body, mesh=mesh, in_specs=in_specs, out_specs=out_specs, check_vma=False)
```

```python
import jax
import jax.numpy as jnp
from jax import lax
from jax.experimental import pallas as pl
from jax.experimental.pallas import tpu as pltpu
from jax.sharding import PartitionSpec as P

HEADS = 4
RADIUS = 4


EPSILON = 1e-06


def shifted(value, axis, steps):
    count = lax.axis_size(axis)
    initial, last = (max(0, -steps), min(count, count - steps))
    return lax.ppermute(value, axis, [(source, source + steps) for source in range(initial, last)])


def with_halo(block, sides, width):
    for axis, dim in sides:
        count = lax.axis_size(axis)
        forward = [(i, i + 1) for i in range(count - 1)]
        backward = [(target, source) for source, target in forward]
        low = lax.ppermute(
            lax.slice_in_dim(block, block.shape[dim] - width, None, axis=dim), axis, forward
        )
        high = lax.ppermute(lax.slice_in_dim(block, 0, width, axis=dim), axis, backward)
        block = jnp.concatenate([low, block, high], axis=dim)
    return block


def convolve(padded, kernel, row_count, col_count):
    nframes = padded.shape[0]
    summed = jnp.zeros((nframes * row_count * col_count, kernel.shape[3]), jnp.float32)
    for tap_row in range(3):
        for tap_col in range(3):
            patch = padded[:, tap_row : tap_row + row_count, tap_col : tap_col + col_count]
            summed = summed + jnp.dot(
                patch.reshape(-1, patch.shape[3]),
                kernel[tap_row, tap_col],
                preferred_element_type=jnp.float32,
            )
    return summed.reshape(nframes, row_count, col_count, -1)


def correlate(current, windowed):
    nframes, tile_rows, tile_cols, channels = current.shape
    span = 2 * RADIUS + 1
    reach = tile_cols + 2 * RADIUS
    col_here = jnp.arange(tile_cols)[:, None, None]
    col_there = jnp.arange(reach)[None, :, None]
    offsets = jnp.arange(span)[None, None, :]
    band = col_there == col_here + offsets
    band_f32 = band.astype(jnp.float32)
    band_bf16 = band.astype(jnp.bfloat16)
    pieces = []
    for shift_row in range(span):
        rows_window = windowed[:, shift_row : shift_row + tile_rows]
        banded = jnp.einsum(
            "fhic,fhjc->fhij", current, rows_window, preferred_element_type=jnp.float32
        )
        pieces.append(
            jnp.einsum("fhij,ijb->fhib", banded, band_f32, precision=lax.Precision.HIGHEST)
        )
    scores = jnp.concatenate(pieces, axis=-1) * channels ** (-0.5)
    top = jnp.max(scores, axis=-1, keepdims=True)
    expo = jnp.exp(scores - top)
    probs = (expo / jnp.sum(expo, axis=-1, keepdims=True)).astype(jnp.bfloat16)
    gathered = jnp.zeros(current.shape, jnp.float32)
    for shift_row in range(span):
        rows_window = windowed[:, shift_row : shift_row + tile_rows]
        chosen = probs[..., shift_row * span : (shift_row + 1) * span]
        spread = jnp.einsum(
            "fhib,ijb->fhij", chosen, band_bf16, preferred_element_type=jnp.float32
        ).astype(jnp.bfloat16)
        gathered = gathered + jnp.einsum(
            "fhij,fhjc->fhic", spread, rows_window, preferred_element_type=jnp.float32
        )
    return (current.astype(jnp.float32) + gathered).astype(jnp.bfloat16)


def project(series, norm_attn, qkv_weight):
    npos, nframes, channels = series.shape
    base = series.astype(jnp.float32)
    normed = (
        base * lax.rsqrt(jnp.mean(base * base, axis=-1, keepdims=True) + EPSILON) * norm_attn
    ).astype(jnp.bfloat16)
    projected = jnp.dot(
        normed.reshape(-1, channels), qkv_weight, preferred_element_type=jnp.float32
    ).astype(jnp.bfloat16)
    projected = projected.reshape(npos, nframes, 3 * channels)
    return (
        projected[..., :channels],
        projected[..., channels : 2 * channels],
        projected[..., 2 * channels :],
    )


def attend(queries, key_rows, value_rows, query_ids, key_ids):
    npos, query_count, channels = queries.shape
    key_count = key_rows.shape[1]
    depth = channels // HEADS
    query_heads = queries.reshape(npos, query_count, HEADS, depth)
    key_heads = key_rows.reshape(npos, key_count, HEADS, depth)
    value_heads = value_rows.reshape(npos, key_count, HEADS, depth)
    scores = jnp.einsum(
        "pqhd,pkhd->phqk", query_heads, key_heads, preferred_element_type=jnp.float32
    ) * depth ** (-0.5)
    allowed = key_ids[None, :] <= query_ids[:, None]
    scores = jnp.where(allowed, scores, -1e30)
    top = jnp.max(scores, axis=-1, keepdims=True)
    expo = jnp.exp(scores - top)
    weights = (expo / jnp.sum(expo, axis=-1, keepdims=True)).astype(jnp.bfloat16)
    attended = jnp.einsum(
        "phqk,pkhd->pqhd", weights, value_heads, preferred_element_type=jnp.float32
    )
    return attended.reshape(npos, query_count, channels).astype(jnp.bfloat16)


def finish(series, attended, out_weight, norm_mlp, mlp_in, mlp_out):
    npos, nframes, channels = series.shape
    resid = series.astype(jnp.float32) + jnp.dot(
        attended.reshape(-1, channels), out_weight, preferred_element_type=jnp.float32
    ).reshape(npos, nframes, channels)
    mlp_input = (
        resid * lax.rsqrt(jnp.mean(resid * resid, axis=-1, keepdims=True) + EPSILON) * norm_mlp
    ).astype(jnp.bfloat16)
    mlp_hidden = jax.nn.gelu(
        jnp.dot(mlp_input.reshape(-1, channels), mlp_in, preferred_element_type=jnp.float32)
    ).astype(jnp.bfloat16)
    output = resid + jnp.dot(mlp_hidden, mlp_out, preferred_element_type=jnp.float32).reshape(
        npos, nframes, channels
    )
    return output.astype(jnp.bfloat16)


def shards(
    frames,
    conv_first,
    conv_second,
    norm_attn,
    qkv_weight,
    out_weight,
    norm_mlp,
    mlp_in,
    mlp_out,
    target,
):
    frame_count, tile_rows, tile_cols, channels = frames.shape
    arrival = shifted(frames, "tm", -1)
    following = jnp.concatenate([frames[1:], arrival], axis=0)
    windowed = with_halo(following, (("ha", 1), ("wa", 2)), RADIUS)
    blended = correlate(frames, windowed)
    padded_first = with_halo(blended, (("ha", 1), ("wa", 2)), 1)
    hidden_map = jax.nn.gelu(convolve(padded_first, conv_first, tile_rows, tile_cols)).astype(
        jnp.bfloat16
    )
    hidden_map = with_halo(hidden_map, (("ha", 1), ("wa", 2)), 1)
    encoded = (
        blended.astype(jnp.float32) + convolve(hidden_map, conv_second, tile_rows, tile_cols)
    ).astype(jnp.bfloat16)
    series = jnp.transpose(
        lax.all_to_all(encoded, "tm", split_axis=1, concat_axis=0, tiled=True), (1, 2, 0, 3)
    )
    layout = series.shape
    tokens_flat = series.reshape(-1, layout[2], layout[3])
    frame_ids = jnp.arange(layout[2])
    queries, key_rows, value_rows = project(tokens_flat, norm_attn, qkv_weight)
    attended = attend(queries, key_rows, value_rows, frame_ids, frame_ids)
    predicted = finish(tokens_flat, attended, out_weight, norm_mlp, mlp_in, mlp_out).reshape(layout)
    errors = predicted.astype(jnp.float32) - target.astype(jnp.float32)
    summed = lax.psum(jnp.sum(errors * errors), ("tm", "ha", "wa"))
    entries = predicted.size * lax.axis_size("tm") * lax.axis_size("ha") * lax.axis_size("wa")
    return (predicted, summed / entries)


RIMS = (2, RADIUS + 2)
SIDE = 16
QROWS = 20
QCOLS = 16


def window_parts(frame, place, tile_rows, tile_cols):
    rim = RIMS[frame]
    main = tile_rows // 2 + rim
    if place == 0:
        rows = [(0, main, rim, 0), (tile_rows - rim, rim, 0, -1)]
    else:
        rows = [(tile_rows - main, main, 0, 0), (0, rim, main, 1)]
    cols = [
        (0, tile_cols, SIDE, 0),
        (tile_cols - SIDE, SIDE, 0, -1),
        (0, SIDE, SIDE + tile_cols, 1),
    ]
    return [(row, col) for row in rows for col in cols]


def gather_kernel(
    ha_count, wa_count, frames_ref, win0, win1, send_sem, recv_sem
):
    wins = (win0, win1)
    _, tile_rows, tile_cols, _ = frames_ref.shape
    here_t, here_a, here_w = (lax.axis_index(n) for n in ("tm", "ha", "wa"))
    barrier = pltpu.get_barrier_semaphore()

    def inside(a, w):
        return (a >= 0) & (a < ha_count) & (w >= 0) & (w < wa_count)

    def device(t, a, w):
        wrapped = (lax.rem(a + ha_count, ha_count), lax.rem(w + wa_count, wa_count))
        return (jnp.int32(t), *wrapped)

    def branch(mine):
        other = 1 - mine
        expected = jnp.int32(0)
        for frame in range(2):
            for row, col in window_parts(frame, mine, tile_rows, tile_cols):
                a, w = here_a + row[3], here_w + col[3]
                if frame == mine and row[3] == 0 and col[3] == 0:
                    continue
                if frame == other and col[3] != 0:
                    continue

                @pl.when(inside(a, w))
                def _():
                    pl.semaphore_signal(
                        barrier,
                        inc=1,
                        device_id=device(frame, a, w),
                        device_id_type=pl.DeviceIdType.MESH,
                    )

        sends = []
        for place in range(2):
            for slot, (row, col) in enumerate(
                window_parts(mine, place, tile_rows, tile_cols)
            ):
                a, w = here_a - row[3], here_w - col[3]
                if place == other and col[3] != 0:
                    continue
                local = place == mine and row[3] == 0 and col[3] == 0
                source = frames_ref.at[0, pl.ds(row[0], row[1]), pl.ds(col[0], col[1])]
                target = wins[mine].at[pl.ds(row[2], row[1]), pl.ds(col[2], col[1])]
                if local:
                    own = pltpu.make_async_copy(source, target, recv_sem.at[mine * 6 + slot])
                    continue
                expected = expected + inside(a, w).astype(jnp.int32)
                sends.append(
                    (
                        inside(a, w),
                        pltpu.make_async_remote_copy(
                            src_ref=source,
                            dst_ref=target,
                            send_sem=send_sem.at[place * 6 + slot],
                            recv_sem=recv_sem.at[mine * 6 + slot],
                            device_id=device(place, a, w),
                            device_id_type=pl.DeviceIdType.MESH,
                        ),
                    )
                )
        own.start()
        arrivals, firsts, passed = [], [], []
        for frame in range(2):
            for slot, (row, col) in enumerate(
                window_parts(frame, mine, tile_rows, tile_cols)
            ):
                a, w = here_a + row[3], here_w + col[3]
                if frame == mine and row[3] == 0 and col[3] == 0:
                    continue
                target = wins[frame].at[pl.ds(row[2], row[1]), pl.ds(col[2], col[1])]

                def clear(target=target):
                    target[...] = jnp.zeros(target.shape, target.dtype)

                arrival = pltpu.make_async_remote_copy(
                    src_ref=target,
                    dst_ref=target,
                    send_sem=send_sem.at[frame * 6 + slot],
                    recv_sem=recv_sem.at[frame * 6 + slot],
                    device_id=device(other, here_a, here_w),
                    device_id_type=pl.DeviceIdType.MESH,
                )
                arrivals.append((inside(a, w), arrival))
                if frame == other and col[3] == 0:
                    firsts.append(arrivals.pop())
                elif frame == other:
                    out = (pl.ds(row[2], row[1]), pl.ds(SIDE + col[0], col[1]))
                    onward = pltpu.make_async_remote_copy(
                        src_ref=wins[frame].at[out],
                        dst_ref=target,
                        send_sem=send_sem.at[frame * 6 + slot],
                        recv_sem=recv_sem.at[frame * 6 + slot],
                        device_id=device(mine, here_a, here_w - col[3]),
                        device_id_type=pl.DeviceIdType.MESH,
                    )
                    passed.append((row[3] != 0, inside(a, here_w - col[3]), onward))
                pl.when(jnp.logical_not(inside(a, w)))(clear)
        pl.semaphore_wait(barrier, expected)
        for exists, copy in sends:
            pl.when(exists)(copy.start)
        own.wait()
        for rim, (exists, arrival) in enumerate(firsts):
            pl.when(exists)(arrival.wait_recv)
            for of_rim, wanted, onward in passed:
                if of_rim == bool(rim):
                    pl.when(wanted)(onward.start)
        for exists, arrival in arrivals:
            pl.when(exists)(arrival.wait_recv)
        for exists, copy in sends + [entry[1:] for entry in passed]:
            pl.when(exists)(copy.wait_send)

    pl.when(here_t == 0)(lambda: branch(0))
    pl.when(here_t == 1)(lambda: branch(1))


def gather_windows(frames):
    _, tile_rows, tile_cols, channels = frames.shape
    shapes = [
        jax.ShapeDtypeStruct(
            (tile_rows // 2 + 2 * rim, tile_cols + 2 * SIDE, channels), frames.dtype
        )
        for rim in RIMS
    ]
    ha_count, wa_count = lax.axis_size("ha"), lax.axis_size("wa")

    def kernel(*refs):
        gather_kernel(ha_count, wa_count, *refs)

    return pl.pallas_call(
        kernel,
        out_shape=shapes,
        in_specs=[pl.BlockSpec(memory_space=pl.ANY)],
        out_specs=[pl.BlockSpec(memory_space=pltpu.VMEM)] * 2,
        scratch_shapes=[
            pltpu.SemaphoreType.DMA((12,)),
            pltpu.SemaphoreType.DMA((12,)),
        ],
        compiler_params=pltpu.CompilerParams(collective_id=0, has_side_effects=True),
    )(frames)


def rounded(value):
    return value.astype(jnp.bfloat16)


def predict_kernel(
    ha_count,
    wa_count,
    win0,
    win1,
    conv_first,
    conv_second,
    norm_attn,
    qkv_weight,
    out_weight,
    norm_mlp,
    mlp_in,
    mlp_out,
    target,
    predicted,
    loss,
    bias,
    blended,
    patches,
    hidden,
    patches_hidden,
    encoded,
    paired,
):
    row_count = win0.shape[0] - 2 * RIMS[0]
    width = win0.shape[1]
    col_count = width - 2 * SIDE
    channels = win0.shape[2]
    here_t, here_a, here_w = (lax.axis_index(n) for n in ("tm", "ha", "wa"))
    first_row = (here_a * 2 + here_t) * row_count
    first_col = here_w * col_count
    image_rows = ha_count * 2 * row_count
    image_cols = wa_count * col_count

    def in_image(shape, row_start, col_start):
        row = lax.broadcasted_iota(jnp.int32, shape, 0) + row_start
        col = lax.broadcasted_iota(jnp.int32, shape, 1) + col_start
        return (row >= 0) & (row < image_rows) & (col >= 0) & (col < image_cols)

    krows, kcols = QROWS + 2 * RADIUS, QCOLS + 16
    queries_n, keys_n = QROWS * QCOLS, krows * kcols
    q_at = lax.broadcasted_iota(jnp.int32, (queries_n, keys_n), 0)
    k_at = lax.broadcasted_iota(jnp.int32, (queries_n, keys_n), 1)
    d_row = k_at // kcols - q_at // QCOLS
    d_col = k_at % kcols - q_at % QCOLS - (8 - RADIUS)
    near = (d_row >= 0) & (d_row <= 2 * RADIUS) & (d_col >= 0) & (d_col <= 2 * RADIUS)
    bias[...] = jnp.where(near, 0.0, -1e30)
    scale = channels ** (-0.5) * 1.4426950408889634

    @pl.loop(0, win0.shape[0] // QROWS)
    def _(step):
        top_row = step * QROWS
        for start in range(8, width - 8, QCOLS):
            query = win0[pl.ds(top_row, QROWS), start : start + QCOLS].reshape(
                queries_n, channels
            )
            keys = win1[pl.ds(top_row, krows), start - 8 : start + QCOLS + 8].reshape(
                keys_n, channels
            )
            scores = lax.dot_general(
                query, keys, (((1,), (1,)), ((), ())), preferred_element_type=jnp.float32
            )
            scores = scores * scale + bias[...]
            expo = jnp.exp2(scores - jnp.max(scores, axis=-1, keepdims=True))
            total = jnp.sum(expo, axis=-1, keepdims=True)
            found = jnp.dot(rounded(expo), keys, preferred_element_type=jnp.float32) / total
            mixed = rounded(query.astype(jnp.float32) + found).astype(jnp.float32)
            mixed = mixed.reshape(QROWS, QCOLS, channels)
            keep = in_image(
                mixed.shape, first_row - RIMS[0] + top_row, first_col - SIDE + start
            )
            blended[pl.ds(top_row, QROWS), start : start + QCOLS] = jnp.where(keep, mixed, 0.0)

    for frame in range(2):
        if frame == 1:
            gap = RIMS[1] - RIMS[0]
            blended[...] = win1[gap : gap + win0.shape[0]].astype(jnp.float32)
        for tap in range(3):
            patches[:, :, tap * channels : (tap + 1) * channels] = rounded(
                blended[:, 7 + tap : width - 9 + tap]
            )

        @pl.loop(0, (row_count + 2) // 9)
        def _(step):
            at = step * 9
            lhs = jnp.concatenate([patches[pl.ds(at + i, 9)] for i in range(3)], axis=-1)
            shape = (9, width - 16, channels)
            out = jnp.dot(
                lhs.reshape(-1, 9 * channels), conv_first[...], preferred_element_type=jnp.float32
            )
            out = rounded(jax.nn.gelu(out)).astype(jnp.float32).reshape(shape)
            keep = in_image(shape, first_row - 1 + at, first_col - 8)
            hidden[pl.ds(at, 9)] = jnp.where(keep, out, 0.0)

        for tap in range(3):
            patches_hidden[:, :, tap * channels : (tap + 1) * channels] = rounded(
                hidden[:, 7 + tap : 7 + tap + col_count]
            )

        @pl.loop(0, row_count // 8)
        def _(step):
            at = step * 8
            lhs = jnp.concatenate([patches_hidden[pl.ds(at + i, 8)] for i in range(3)], axis=-1)
            out = jnp.dot(
                lhs.reshape(-1, 9 * channels), conv_second[...], preferred_element_type=jnp.float32
            )
            base = blended[pl.ds(at + 2, 8), SIDE : SIDE + col_count].reshape(out.shape)
            encoded[frame, pl.ds(at * col_count, 8 * col_count)] = rounded(base + out).astype(
                jnp.float32
            )

    depth = channels // HEADS
    lane_in = lax.broadcasted_iota(jnp.int32, (2 * channels, channels), 0) % channels
    lane_out = lax.broadcasted_iota(jnp.int32, (2 * channels, channels), 1)
    head_sum = rounded(jnp.where(lane_in // depth == lane_out // depth, 1.0, 0.0))
    chunk = 1024

    def unit(value, gain):
        mean = jnp.mean(value * value, axis=-1, keepdims=True)
        return rounded(value * lax.rsqrt(mean + EPSILON) * gain[...])

    def dot(left, right):
        return jnp.dot(left, right, preferred_element_type=jnp.float32)

    @pl.loop(0, row_count * col_count // chunk, init_carry=jnp.zeros((8, channels), jnp.float32))
    def errors(step, carry):
        at = pl.multiple_of(step * chunk, chunk)
        series = jnp.concatenate([encoded[0, pl.ds(at, chunk)], encoded[1, pl.ds(at, chunk)]])
        projected = rounded(dot(unit(series, norm_attn), qkv_weight[...])).astype(jnp.float32)
        query = projected[chunk:, :channels]
        keys = projected[:, channels : 2 * channels]
        values = projected[:, 2 * channels :]
        product = query * (keys[chunk:] - keys[:chunk])
        high = rounded(product)
        low = rounded(product - high.astype(jnp.float32))
        gap = dot(jnp.concatenate([high, low], axis=-1), head_sum) * depth ** (-0.5)
        half = 0.5 * jnp.tanh(0.5 * gap)
        weight_now = rounded(0.5 + half).astype(jnp.float32)
        weight_past = rounded(0.5 - half).astype(jnp.float32)
        attended = weight_past * values[:chunk] + weight_now * values[chunk:]
        attended = rounded(jnp.concatenate([values[:chunk], attended]))
        resid = series + dot(attended, out_weight[...])
        inner = rounded(jax.nn.gelu(dot(unit(resid, norm_mlp), mlp_in[...])))
        output = resid + dot(inner, mlp_out[...])
        paired[pl.ds(0, chunk, stride=2)] = output[:chunk]
        paired[pl.ds(1, chunk, stride=2)] = output[chunk:]
        final = rounded(paired[...])
        both = pl.ds(pl.multiple_of(2 * at, 2 * chunk), 2 * chunk)
        predicted[both] = final
        error = final.astype(jnp.float32) - target[both].astype(jnp.float32)
        return carry + jnp.sum((error * error).reshape(-1, 8, channels), axis=0)

    loss[...] = errors


def predict(win0, win1, weights, target):
    row_count = win0.shape[0] - 2 * RIMS[0]
    width, channels = win0.shape[1:]
    col_count = width - 2 * SIDE
    ha_count, wa_count = lax.axis_size("ha"), lax.axis_size("wa")

    def kernel(*refs):
        predict_kernel(ha_count, wa_count, *refs)

    tokens = 2 * row_count * col_count
    operands = (win0, win1, *weights, target)
    return pl.pallas_call(
        kernel,
        out_shape=[
            jax.ShapeDtypeStruct((tokens, channels), jnp.bfloat16),
            jax.ShapeDtypeStruct((8, channels), jnp.float32),
        ],
        in_specs=[pl.BlockSpec(memory_space=pltpu.VMEM)] * len(operands),
        out_specs=[pl.BlockSpec(memory_space=pltpu.VMEM)] * 2,
        scratch_shapes=[
            pltpu.VMEM((QROWS * QCOLS, (QROWS + 2 * RADIUS) * (QCOLS + 16)), jnp.float32),
            pltpu.VMEM((row_count + 4, width, channels), jnp.float32),
            pltpu.VMEM((row_count + 4, width - 16, 3 * channels), jnp.bfloat16),
            pltpu.VMEM((row_count + 2, width - 16, channels), jnp.float32),
            pltpu.VMEM((row_count + 2, col_count, 3 * channels), jnp.bfloat16),
            pltpu.VMEM((2, row_count * col_count, channels), jnp.float32),
            pltpu.VMEM((2048, channels), jnp.float32),
        ],
        compiler_params=pltpu.CompilerParams(vmem_limit_bytes=60 * 1024 * 1024),
    )(*operands)


def total_kernel(
    wa_count, ha_count, near_count, scale, errors, total, near, part, far, near_sems, far_sems
):
    here_t, here_a, here_w = (lax.axis_index(n) for n in ("tm", "ha", "wa"))
    here = here_t * wa_count + here_w

    def near_peer(step):
        slot = lax.rem(here + step, near_count)
        return slot, (slot // wa_count, here_a, lax.rem(slot, wa_count))

    def far_peer(step):
        slot = lax.rem(here_a + step, ha_count)
        return slot, (here_t, slot, here_w)

    barrier = pltpu.get_barrier_semaphore()
    groups = ((near_peer, near_count), (far_peer, ha_count))
    for peer, count in groups:
        for step in range(1, count):
            pl.semaphore_signal(
                barrier,
                inc=1,
                device_id=peer(step)[1],
                device_id_type=pl.DeviceIdType.MESH,
            )
    pl.semaphore_wait(barrier, near_count + ha_count - 2)

    def exchange(source, slots, sems, peer, count, own):
        def copy(step, slot, device):
            return pltpu.make_async_remote_copy(
                src_ref=source,
                dst_ref=slots.at[slot],
                send_sem=sems.at[0, step],
                recv_sem=sems.at[1, slot],
                device_id=device,
                device_id_type=pl.DeviceIdType.MESH,
            )

        for step in range(1, count):
            copy(step, own, peer(step)[1]).start()
        slots[own] = source[...]
        for step in range(1, count):
            slot, device = peer(step)
            copy(step, slot, device).wait_recv()
        for step in range(1, count):
            copy(step, own, peer(step)[1]).wait_send()
        summed = slots[0]
        for slot in range(1, count):
            summed = summed + slots[slot]
        return summed

    part[...] = exchange(errors, near, near_sems, near_peer, near_count, here)
    summed = exchange(part, far, far_sems, far_peer, ha_count, here_a)
    total[0, 0] = jnp.sum(summed) * scale


def total_error(errors, entries):
    ha_count, wa_count = lax.axis_size("ha"), lax.axis_size("wa")
    near_count = lax.axis_size("tm") * wa_count

    def kernel(*refs):
        total_kernel(wa_count, ha_count, near_count, 1.0 / entries, *refs)

    return pl.pallas_call(
        kernel,
        out_shape=jax.ShapeDtypeStruct((1, 1), jnp.float32),
        in_specs=[pl.BlockSpec(memory_space=pltpu.VMEM)],
        out_specs=pl.BlockSpec(memory_space=pltpu.SMEM),
        scratch_shapes=[
            pltpu.VMEM((near_count, *errors.shape), jnp.float32),
            pltpu.VMEM(errors.shape, jnp.float32),
            pltpu.VMEM((ha_count, *errors.shape), jnp.float32),
            pltpu.SemaphoreType.DMA((2, near_count)),
            pltpu.SemaphoreType.DMA((2, ha_count)),
        ],
        compiler_params=pltpu.CompilerParams(collective_id=1, has_side_effects=True),
    )(errors)


def pair_shards(
    frames,
    conv_first,
    conv_second,
    norm_attn,
    qkv_weight,
    out_weight,
    norm_mlp,
    mlp_in,
    mlp_out,
    target,
):
    channels = frames.shape[3]
    win0, win1 = gather_windows(frames)
    weights = (
        conv_first.reshape(-1, channels),
        conv_second.reshape(-1, channels),
        norm_attn.reshape(1, channels),
        qkv_weight,
        out_weight,
        norm_mlp.reshape(1, channels),
        mlp_in,
        mlp_out,
    )
    predicted, errors = predict(win0, win1, weights, target.reshape(-1, channels))
    entries = target.size * lax.axis_size("tm") * lax.axis_size("ha") * lax.axis_size("wa")
    return (predicted.reshape(target.shape), total_error(errors, entries).reshape(()))


def solution(mesh):
    in_specs = (
        P("tm", "ha", "wa", None),
        P(),
        P(),
        P(),
        P(),
        P(),
        P(),
        P(),
        P(),
        P(("ha", "tm"), "wa", None, None),
    )
    out_specs = (P(("ha", "tm"), "wa", None, None), P())
    body = pair_shards if mesh.shape["tm"] == 2 else shards
    return jax.shard_map(body, mesh=mesh, in_specs=in_specs, out_specs=out_specs, check_vma=False)
```

```python
import jax
import jax.numpy as jnp
from jax import lax
from jax.experimental import pallas as pl
from jax.experimental.pallas import tpu as pltpu
from jax.sharding import PartitionSpec as P

HEADS = 4
RADIUS = 4


EPSILON = 1e-06


def shifted(value, axis, steps):
    count = lax.axis_size(axis)
    initial, last = (max(0, -steps), min(count, count - steps))
    return lax.ppermute(value, axis, [(source, source + steps) for source in range(initial, last)])


def with_halo(block, sides, width):
    for axis, dim in sides:
        count = lax.axis_size(axis)
        forward = [(i, i + 1) for i in range(count - 1)]
        backward = [(target, source) for source, target in forward]
        low = lax.ppermute(
            lax.slice_in_dim(block, block.shape[dim] - width, None, axis=dim), axis, forward
        )
        high = lax.ppermute(lax.slice_in_dim(block, 0, width, axis=dim), axis, backward)
        block = jnp.concatenate([low, block, high], axis=dim)
    return block


def convolve(padded, kernel, row_count, col_count):
    nframes = padded.shape[0]
    summed = jnp.zeros((nframes * row_count * col_count, kernel.shape[3]), jnp.float32)
    for tap_row in range(3):
        for tap_col in range(3):
            patch = padded[:, tap_row : tap_row + row_count, tap_col : tap_col + col_count]
            summed = summed + jnp.dot(
                patch.reshape(-1, patch.shape[3]),
                kernel[tap_row, tap_col],
                preferred_element_type=jnp.float32,
            )
    return summed.reshape(nframes, row_count, col_count, -1)


def correlate(current, windowed):
    nframes, tile_rows, tile_cols, channels = current.shape
    span = 2 * RADIUS + 1
    reach = tile_cols + 2 * RADIUS
    col_here = jnp.arange(tile_cols)[:, None, None]
    col_there = jnp.arange(reach)[None, :, None]
    offsets = jnp.arange(span)[None, None, :]
    band = col_there == col_here + offsets
    band_f32 = band.astype(jnp.float32)
    band_bf16 = band.astype(jnp.bfloat16)
    pieces = []
    for shift_row in range(span):
        rows_window = windowed[:, shift_row : shift_row + tile_rows]
        banded = jnp.einsum(
            "fhic,fhjc->fhij", current, rows_window, preferred_element_type=jnp.float32
        )
        pieces.append(
            jnp.einsum("fhij,ijb->fhib", banded, band_f32, precision=lax.Precision.HIGHEST)
        )
    scores = jnp.concatenate(pieces, axis=-1) * channels ** (-0.5)
    top = jnp.max(scores, axis=-1, keepdims=True)
    expo = jnp.exp(scores - top)
    probs = (expo / jnp.sum(expo, axis=-1, keepdims=True)).astype(jnp.bfloat16)
    gathered = jnp.zeros(current.shape, jnp.float32)
    for shift_row in range(span):
        rows_window = windowed[:, shift_row : shift_row + tile_rows]
        chosen = probs[..., shift_row * span : (shift_row + 1) * span]
        spread = jnp.einsum(
            "fhib,ijb->fhij", chosen, band_bf16, preferred_element_type=jnp.float32
        ).astype(jnp.bfloat16)
        gathered = gathered + jnp.einsum(
            "fhij,fhjc->fhic", spread, rows_window, preferred_element_type=jnp.float32
        )
    return (current.astype(jnp.float32) + gathered).astype(jnp.bfloat16)


def project(series, norm_attn, qkv_weight):
    npos, nframes, channels = series.shape
    base = series.astype(jnp.float32)
    normed = (
        base * lax.rsqrt(jnp.mean(base * base, axis=-1, keepdims=True) + EPSILON) * norm_attn
    ).astype(jnp.bfloat16)
    projected = jnp.dot(
        normed.reshape(-1, channels), qkv_weight, preferred_element_type=jnp.float32
    ).astype(jnp.bfloat16)
    projected = projected.reshape(npos, nframes, 3 * channels)
    return (
        projected[..., :channels],
        projected[..., channels : 2 * channels],
        projected[..., 2 * channels :],
    )


def attend(queries, key_rows, value_rows, query_ids, key_ids):
    npos, query_count, channels = queries.shape
    key_count = key_rows.shape[1]
    depth = channels // HEADS
    query_heads = queries.reshape(npos, query_count, HEADS, depth)
    key_heads = key_rows.reshape(npos, key_count, HEADS, depth)
    value_heads = value_rows.reshape(npos, key_count, HEADS, depth)
    scores = jnp.einsum(
        "pqhd,pkhd->phqk", query_heads, key_heads, preferred_element_type=jnp.float32
    ) * depth ** (-0.5)
    allowed = key_ids[None, :] <= query_ids[:, None]
    scores = jnp.where(allowed, scores, -1e30)
    top = jnp.max(scores, axis=-1, keepdims=True)
    expo = jnp.exp(scores - top)
    weights = (expo / jnp.sum(expo, axis=-1, keepdims=True)).astype(jnp.bfloat16)
    attended = jnp.einsum(
        "phqk,pkhd->pqhd", weights, value_heads, preferred_element_type=jnp.float32
    )
    return attended.reshape(npos, query_count, channels).astype(jnp.bfloat16)


def finish(series, attended, out_weight, norm_mlp, mlp_in, mlp_out):
    npos, nframes, channels = series.shape
    resid = series.astype(jnp.float32) + jnp.dot(
        attended.reshape(-1, channels), out_weight, preferred_element_type=jnp.float32
    ).reshape(npos, nframes, channels)
    mlp_input = (
        resid * lax.rsqrt(jnp.mean(resid * resid, axis=-1, keepdims=True) + EPSILON) * norm_mlp
    ).astype(jnp.bfloat16)
    mlp_hidden = jax.nn.gelu(
        jnp.dot(mlp_input.reshape(-1, channels), mlp_in, preferred_element_type=jnp.float32)
    ).astype(jnp.bfloat16)
    output = resid + jnp.dot(mlp_hidden, mlp_out, preferred_element_type=jnp.float32).reshape(
        npos, nframes, channels
    )
    return output.astype(jnp.bfloat16)


def shards(
    frames,
    conv_first,
    conv_second,
    norm_attn,
    qkv_weight,
    out_weight,
    norm_mlp,
    mlp_in,
    mlp_out,
    target,
):
    frame_count, tile_rows, tile_cols, channels = frames.shape
    arrival = shifted(frames, "tm", -1)
    following = jnp.concatenate([frames[1:], arrival], axis=0)
    windowed = with_halo(following, (("ha", 1), ("wa", 2)), RADIUS)
    blended = correlate(frames, windowed)
    padded_first = with_halo(blended, (("ha", 1), ("wa", 2)), 1)
    hidden_map = jax.nn.gelu(convolve(padded_first, conv_first, tile_rows, tile_cols)).astype(
        jnp.bfloat16
    )
    hidden_map = with_halo(hidden_map, (("ha", 1), ("wa", 2)), 1)
    encoded = (
        blended.astype(jnp.float32) + convolve(hidden_map, conv_second, tile_rows, tile_cols)
    ).astype(jnp.bfloat16)
    series = jnp.transpose(
        lax.all_to_all(encoded, "tm", split_axis=1, concat_axis=0, tiled=True), (1, 2, 0, 3)
    )
    layout = series.shape
    tokens_flat = series.reshape(-1, layout[2], layout[3])
    frame_ids = jnp.arange(layout[2])
    queries, key_rows, value_rows = project(tokens_flat, norm_attn, qkv_weight)
    attended = attend(queries, key_rows, value_rows, frame_ids, frame_ids)
    predicted = finish(tokens_flat, attended, out_weight, norm_mlp, mlp_in, mlp_out).reshape(layout)
    errors = predicted.astype(jnp.float32) - target.astype(jnp.float32)
    summed = lax.psum(jnp.sum(errors * errors), ("tm", "ha", "wa"))
    entries = predicted.size * lax.axis_size("tm") * lax.axis_size("ha") * lax.axis_size("wa")
    return (predicted, summed / entries)


RIMS = (2, RADIUS + 2)
SIDE = 16
QROWS = 20
QCOLS = 16


def window_parts(frame, place, tile_rows, tile_cols):
    rim = RIMS[frame]
    main = tile_rows // 2 + rim
    if place == 0:
        rows = [(0, main, rim, 0), (tile_rows - rim, rim, 0, -1)]
    else:
        rows = [(tile_rows - main, main, 0, 0), (0, rim, main, 1)]
    cols = [
        (0, tile_cols, SIDE, 0),
        (tile_cols - SIDE, SIDE, 0, -1),
        (0, SIDE, SIDE + tile_cols, 1),
    ]
    return [(row, col) for row in rows for col in cols]


def gather_kernel(
    ha_count, wa_count, frames_ref, win0, win1, send_sem, recv_sem
):
    wins = (win0, win1)
    _, tile_rows, tile_cols, _ = frames_ref.shape
    here_t, here_a, here_w = (lax.axis_index(n) for n in ("tm", "ha", "wa"))
    barrier = pltpu.get_barrier_semaphore()

    def inside(a, w):
        return (a >= 0) & (a < ha_count) & (w >= 0) & (w < wa_count)

    def device(t, a, w):
        wrapped = (lax.rem(a + ha_count, ha_count), lax.rem(w + wa_count, wa_count))
        return (jnp.int32(t), *wrapped)

    def branch(mine):
        other = 1 - mine
        expected = jnp.int32(0)
        for frame in range(2):
            for row, col in window_parts(frame, mine, tile_rows, tile_cols):
                a, w = here_a + row[3], here_w + col[3]
                if frame == mine and row[3] == 0 and col[3] == 0:
                    continue
                if frame == other and col[3] != 0:
                    continue

                @pl.when(inside(a, w))
                def _():
                    pl.semaphore_signal(
                        barrier,
                        inc=1,
                        device_id=device(frame, a, w),
                        device_id_type=pl.DeviceIdType.MESH,
                    )

        sends = []
        for place in (other, mine):
            for slot, (row, col) in enumerate(
                window_parts(mine, place, tile_rows, tile_cols)
            ):
                a, w = here_a - row[3], here_w - col[3]
                if place == other and col[3] != 0:
                    continue
                local = place == mine and row[3] == 0 and col[3] == 0
                source = frames_ref.at[0, pl.ds(row[0], row[1]), pl.ds(col[0], col[1])]
                target = wins[mine].at[pl.ds(row[2], row[1]), pl.ds(col[2], col[1])]
                if local:
                    own = pltpu.make_async_copy(source, target, recv_sem.at[mine * 6 + slot])
                    continue
                expected = expected + inside(a, w).astype(jnp.int32)
                sends.append(
                    (
                        inside(a, w),
                        pltpu.make_async_remote_copy(
                            src_ref=source,
                            dst_ref=target,
                            send_sem=send_sem.at[place * 6 + slot],
                            recv_sem=recv_sem.at[mine * 6 + slot],
                            device_id=device(place, a, w),
                            device_id_type=pl.DeviceIdType.MESH,
                        ),
                    )
                )
        own.start()
        arrivals, firsts, passed = [], [], []
        for frame in range(2):
            for slot, (row, col) in enumerate(
                window_parts(frame, mine, tile_rows, tile_cols)
            ):
                a, w = here_a + row[3], here_w + col[3]
                if frame == mine and row[3] == 0 and col[3] == 0:
                    continue
                target = wins[frame].at[pl.ds(row[2], row[1]), pl.ds(col[2], col[1])]

                def clear(target=target):
                    target[...] = jnp.zeros(target.shape, target.dtype)

                arrival = pltpu.make_async_remote_copy(
                    src_ref=target,
                    dst_ref=target,
                    send_sem=send_sem.at[frame * 6 + slot],
                    recv_sem=recv_sem.at[frame * 6 + slot],
                    device_id=device(other, here_a, here_w),
                    device_id_type=pl.DeviceIdType.MESH,
                )
                arrivals.append((inside(a, w), arrival))
                if frame == other and col[3] == 0:
                    firsts.append(arrivals.pop())
                elif frame == other:
                    out = (pl.ds(row[2], row[1]), pl.ds(SIDE + col[0], col[1]))
                    onward = pltpu.make_async_remote_copy(
                        src_ref=wins[frame].at[out],
                        dst_ref=target,
                        send_sem=send_sem.at[frame * 6 + slot],
                        recv_sem=recv_sem.at[frame * 6 + slot],
                        device_id=device(mine, here_a, here_w - col[3]),
                        device_id_type=pl.DeviceIdType.MESH,
                    )
                    passed.append((row[3] != 0, inside(a, here_w - col[3]), onward))
                pl.when(jnp.logical_not(inside(a, w)))(clear)
        pl.semaphore_wait(barrier, expected)
        for exists, copy in sends:
            pl.when(exists)(copy.start)
        own.wait()
        for rim, (exists, arrival) in enumerate(firsts):
            pl.when(exists)(arrival.wait_recv)
            for of_rim, wanted, onward in passed:
                if of_rim == bool(rim):
                    pl.when(wanted)(onward.start)
        for exists, arrival in arrivals:
            pl.when(exists)(arrival.wait_recv)
        for exists, copy in sends + [entry[1:] for entry in passed]:
            pl.when(exists)(copy.wait_send)

    pl.when(here_t == 0)(lambda: branch(0))
    pl.when(here_t == 1)(lambda: branch(1))


def gather_windows(frames):
    _, tile_rows, tile_cols, channels = frames.shape
    shapes = [
        jax.ShapeDtypeStruct(
            (tile_rows // 2 + 2 * rim, tile_cols + 2 * SIDE, channels), frames.dtype
        )
        for rim in RIMS
    ]
    ha_count, wa_count = lax.axis_size("ha"), lax.axis_size("wa")

    def kernel(*refs):
        gather_kernel(ha_count, wa_count, *refs)

    return pl.pallas_call(
        kernel,
        out_shape=shapes,
        in_specs=[pl.BlockSpec(memory_space=pl.ANY)],
        out_specs=[pl.BlockSpec(memory_space=pltpu.VMEM)] * 2,
        scratch_shapes=[
            pltpu.SemaphoreType.DMA((12,)),
            pltpu.SemaphoreType.DMA((12,)),
        ],
        compiler_params=pltpu.CompilerParams(collective_id=0, has_side_effects=True),
    )(frames)


def rounded(value):
    return value.astype(jnp.bfloat16)


def predict_kernel(
    ha_count,
    wa_count,
    win0,
    win1,
    conv_first,
    conv_second,
    norm_attn,
    qkv_weight,
    out_weight,
    norm_mlp,
    mlp_in,
    mlp_out,
    target,
    predicted,
    loss,
    bias,
    blended,
    patches,
    hidden,
    patches_hidden,
    encoded,
    paired,
):
    row_count = win0.shape[0] - 2 * RIMS[0]
    width = win0.shape[1]
    col_count = width - 2 * SIDE
    channels = win0.shape[2]
    here_t, here_a, here_w = (lax.axis_index(n) for n in ("tm", "ha", "wa"))
    first_row = (here_a * 2 + here_t) * row_count
    first_col = here_w * col_count
    image_rows = ha_count * 2 * row_count
    image_cols = wa_count * col_count

    def in_image(shape, row_start, col_start):
        row = lax.broadcasted_iota(jnp.int32, shape, 0) + row_start
        col = lax.broadcasted_iota(jnp.int32, shape, 1) + col_start
        return (row >= 0) & (row < image_rows) & (col >= 0) & (col < image_cols)

    krows, kcols = QROWS + 2 * RADIUS, QCOLS + 16
    queries_n, keys_n = QROWS * QCOLS, krows * kcols
    q_at = lax.broadcasted_iota(jnp.int32, (queries_n, keys_n), 0)
    k_at = lax.broadcasted_iota(jnp.int32, (queries_n, keys_n), 1)
    d_row = k_at // kcols - q_at // QCOLS
    d_col = k_at % kcols - q_at % QCOLS - (8 - RADIUS)
    near = (d_row >= 0) & (d_row <= 2 * RADIUS) & (d_col >= 0) & (d_col <= 2 * RADIUS)
    bias[...] = jnp.where(near, 0.0, -1e30)
    scale = channels ** (-0.5) * 1.4426950408889634

    @pl.loop(0, win0.shape[0] // QROWS)
    def _(step):
        top_row = step * QROWS
        for start in range(8, width - 8, QCOLS):
            query = win0[pl.ds(top_row, QROWS), start : start + QCOLS].reshape(
                queries_n, channels
            )
            keys = win1[pl.ds(top_row, krows), start - 8 : start + QCOLS + 8].reshape(
                keys_n, channels
            )
            scores = lax.dot_general(
                query, keys, (((1,), (1,)), ((), ())), preferred_element_type=jnp.float32
            )
            scores = scores * scale + bias[...]
            expo = jnp.exp2(scores - jnp.max(scores, axis=-1, keepdims=True))
            total = jnp.sum(expo, axis=-1, keepdims=True)
            found = jnp.dot(rounded(expo), keys, preferred_element_type=jnp.float32) / total
            mixed = rounded(query.astype(jnp.float32) + found).astype(jnp.float32)
            mixed = mixed.reshape(QROWS, QCOLS, channels)
            keep = in_image(
                mixed.shape, first_row - RIMS[0] + top_row, first_col - SIDE + start
            )
            blended[pl.ds(top_row, QROWS), start : start + QCOLS] = jnp.where(keep, mixed, 0.0)

    for frame in range(2):
        if frame == 1:
            gap = RIMS[1] - RIMS[0]
            blended[...] = win1[gap : gap + win0.shape[0]].astype(jnp.float32)
        for tap in range(3):
            patches[:, :, tap * channels : (tap + 1) * channels] = rounded(
                blended[:, 7 + tap : width - 9 + tap]
            )

        @pl.loop(0, (row_count + 2) // 9)
        def _(step):
            at = step * 9
            lhs = jnp.concatenate([patches[pl.ds(at + i, 9)] for i in range(3)], axis=-1)
            shape = (9, width - 16, channels)
            out = jnp.dot(
                lhs.reshape(-1, 9 * channels), conv_first[...], preferred_element_type=jnp.float32
            )
            out = rounded(jax.nn.gelu(out)).astype(jnp.float32).reshape(shape)
            keep = in_image(shape, first_row - 1 + at, first_col - 8)
            hidden[pl.ds(at, 9)] = jnp.where(keep, out, 0.0)

        for tap in range(3):
            patches_hidden[:, :, tap * channels : (tap + 1) * channels] = rounded(
                hidden[:, 7 + tap : 7 + tap + col_count]
            )

        @pl.loop(0, row_count // 8)
        def _(step):
            at = step * 8
            lhs = jnp.concatenate([patches_hidden[pl.ds(at + i, 8)] for i in range(3)], axis=-1)
            out = jnp.dot(
                lhs.reshape(-1, 9 * channels), conv_second[...], preferred_element_type=jnp.float32
            )
            base = blended[pl.ds(at + 2, 8), SIDE : SIDE + col_count].reshape(out.shape)
            encoded[frame, pl.ds(at * col_count, 8 * col_count)] = rounded(base + out).astype(
                jnp.float32
            )

    depth = channels // HEADS
    lane_in = lax.broadcasted_iota(jnp.int32, (2 * channels, channels), 0) % channels
    lane_out = lax.broadcasted_iota(jnp.int32, (2 * channels, channels), 1)
    head_sum = rounded(jnp.where(lane_in // depth == lane_out // depth, 1.0, 0.0))
    chunk = 1024

    def unit(value, gain):
        mean = jnp.mean(value * value, axis=-1, keepdims=True)
        return rounded(value * lax.rsqrt(mean + EPSILON) * gain[...])

    def dot(left, right):
        return jnp.dot(left, right, preferred_element_type=jnp.float32)

    @pl.loop(0, row_count * col_count // chunk, init_carry=jnp.zeros((8, channels), jnp.float32))
    def errors(step, carry):
        at = pl.multiple_of(step * chunk, chunk)
        series = jnp.concatenate([encoded[0, pl.ds(at, chunk)], encoded[1, pl.ds(at, chunk)]])
        projected = rounded(dot(unit(series, norm_attn), qkv_weight[...])).astype(jnp.float32)
        query = projected[chunk:, :channels]
        keys = projected[:, channels : 2 * channels]
        values = projected[:, 2 * channels :]
        product = query * (keys[chunk:] - keys[:chunk])
        high = rounded(product)
        low = rounded(product - high.astype(jnp.float32))
        gap = dot(jnp.concatenate([high, low], axis=-1), head_sum) * depth ** (-0.5)
        half = 0.5 * jnp.tanh(0.5 * gap)
        weight_now = rounded(0.5 + half).astype(jnp.float32)
        weight_past = rounded(0.5 - half).astype(jnp.float32)
        attended = weight_past * values[:chunk] + weight_now * values[chunk:]
        attended = rounded(jnp.concatenate([values[:chunk], attended]))
        resid = series + dot(attended, out_weight[...])
        inner = rounded(jax.nn.gelu(dot(unit(resid, norm_mlp), mlp_in[...])))
        output = resid + dot(inner, mlp_out[...])
        paired[pl.ds(0, chunk, stride=2)] = output[:chunk]
        paired[pl.ds(1, chunk, stride=2)] = output[chunk:]
        final = rounded(paired[...])
        both = pl.ds(pl.multiple_of(2 * at, 2 * chunk), 2 * chunk)
        predicted[both] = final
        error = final.astype(jnp.float32) - target[both].astype(jnp.float32)
        return carry + jnp.sum((error * error).reshape(-1, 8, channels), axis=0)

    loss[...] = errors


def predict(win0, win1, weights, target):
    row_count = win0.shape[0] - 2 * RIMS[0]
    width, channels = win0.shape[1:]
    col_count = width - 2 * SIDE
    ha_count, wa_count = lax.axis_size("ha"), lax.axis_size("wa")

    def kernel(*refs):
        predict_kernel(ha_count, wa_count, *refs)

    tokens = 2 * row_count * col_count
    operands = (win0, win1, *weights, target)
    return pl.pallas_call(
        kernel,
        out_shape=[
            jax.ShapeDtypeStruct((tokens, channels), jnp.bfloat16),
            jax.ShapeDtypeStruct((8, channels), jnp.float32),
        ],
        in_specs=[pl.BlockSpec(memory_space=pltpu.VMEM)] * len(operands),
        out_specs=[pl.BlockSpec(memory_space=pltpu.VMEM)] * 2,
        scratch_shapes=[
            pltpu.VMEM((QROWS * QCOLS, (QROWS + 2 * RADIUS) * (QCOLS + 16)), jnp.float32),
            pltpu.VMEM((row_count + 4, width, channels), jnp.float32),
            pltpu.VMEM((row_count + 4, width - 16, 3 * channels), jnp.bfloat16),
            pltpu.VMEM((row_count + 2, width - 16, channels), jnp.float32),
            pltpu.VMEM((row_count + 2, col_count, 3 * channels), jnp.bfloat16),
            pltpu.VMEM((2, row_count * col_count, channels), jnp.float32),
            pltpu.VMEM((2048, channels), jnp.float32),
        ],
        compiler_params=pltpu.CompilerParams(vmem_limit_bytes=60 * 1024 * 1024),
    )(*operands)


def total_kernel(
    wa_count, ha_count, near_count, scale, errors, total, near, part, far, near_sems, far_sems
):
    here_t, here_a, here_w = (lax.axis_index(n) for n in ("tm", "ha", "wa"))
    here = here_t * wa_count + here_w

    def near_peer(step):
        slot = lax.rem(here + step, near_count)
        return slot, (slot // wa_count, here_a, lax.rem(slot, wa_count))

    def far_peer(step):
        slot = lax.rem(here_a + step, ha_count)
        return slot, (here_t, slot, here_w)

    barrier = pltpu.get_barrier_semaphore()
    groups = ((near_peer, near_count), (far_peer, ha_count))
    for peer, count in groups:
        for step in range(1, count):
            pl.semaphore_signal(
                barrier,
                inc=1,
                device_id=peer(step)[1],
                device_id_type=pl.DeviceIdType.MESH,
            )
    pl.semaphore_wait(barrier, near_count + ha_count - 2)

    def exchange(source, slots, sems, peer, count, own):
        def copy(step, slot, device):
            return pltpu.make_async_remote_copy(
                src_ref=source,
                dst_ref=slots.at[slot],
                send_sem=sems.at[0, step],
                recv_sem=sems.at[1, slot],
                device_id=device,
                device_id_type=pl.DeviceIdType.MESH,
            )

        for step in range(1, count):
            copy(step, own, peer(step)[1]).start()
        slots[own] = source[...]
        for step in range(1, count):
            slot, device = peer(step)
            copy(step, slot, device).wait_recv()
        for step in range(1, count):
            copy(step, own, peer(step)[1]).wait_send()
        summed = slots[0]
        for slot in range(1, count):
            summed = summed + slots[slot]
        return summed

    part[...] = exchange(errors, near, near_sems, near_peer, near_count, here)
    summed = exchange(part, far, far_sems, far_peer, ha_count, here_a)
    total[0, 0] = jnp.sum(summed) * scale


def total_error(errors, entries):
    ha_count, wa_count = lax.axis_size("ha"), lax.axis_size("wa")
    near_count = lax.axis_size("tm") * wa_count

    def kernel(*refs):
        total_kernel(wa_count, ha_count, near_count, 1.0 / entries, *refs)

    return pl.pallas_call(
        kernel,
        out_shape=jax.ShapeDtypeStruct((1, 1), jnp.float32),
        in_specs=[pl.BlockSpec(memory_space=pltpu.VMEM)],
        out_specs=pl.BlockSpec(memory_space=pltpu.SMEM),
        scratch_shapes=[
            pltpu.VMEM((near_count, *errors.shape), jnp.float32),
            pltpu.VMEM(errors.shape, jnp.float32),
            pltpu.VMEM((ha_count, *errors.shape), jnp.float32),
            pltpu.SemaphoreType.DMA((2, near_count)),
            pltpu.SemaphoreType.DMA((2, ha_count)),
        ],
        compiler_params=pltpu.CompilerParams(collective_id=1, has_side_effects=True),
    )(errors)


def pair_shards(
    frames,
    conv_first,
    conv_second,
    norm_attn,
    qkv_weight,
    out_weight,
    norm_mlp,
    mlp_in,
    mlp_out,
    target,
):
    channels = frames.shape[3]
    win0, win1 = gather_windows(frames)
    weights = (
        conv_first.reshape(-1, channels),
        conv_second.reshape(-1, channels),
        norm_attn.reshape(1, channels),
        qkv_weight,
        out_weight,
        norm_mlp.reshape(1, channels),
        mlp_in,
        mlp_out,
    )
    predicted, errors = predict(win0, win1, weights, target.reshape(-1, channels))
    entries = target.size * lax.axis_size("tm") * lax.axis_size("ha") * lax.axis_size("wa")
    return (predicted.reshape(target.shape), total_error(errors, entries).reshape(()))


def solution(mesh):
    in_specs = (
        P("tm", "ha", "wa", None),
        P(),
        P(),
        P(),
        P(),
        P(),
        P(),
        P(),
        P(),
        P(("ha", "tm"), "wa", None, None),
    )
    out_specs = (P(("ha", "tm"), "wa", None, None), P())
    body = pair_shards if mesh.shape["tm"] == 2 else shards
    return jax.shard_map(body, mesh=mesh, in_specs=in_specs, out_specs=out_specs, check_vma=False)
```
